32 devices in a mesh: ex: 8 (over z, core), hid: 4 (over y, x).
Axes of the slice: x: 2, y: 2, z: 4, core: 2. Of those that a mesh axis runs over, the one named last changes fastest.
Arguments:
- tokens: bfloat16 [512, 2048], P(('ex', 'hid')), may hold values from -6 to 6
- cotangent: bfloat16 [512, 2048], P(('ex', 'hid')), may hold values from -6 to 6
- gates: float32 [512, 4], P(('ex', 'hid')), may hold values from 0.1 to 1
- routes: int32 [512, 4], P(('ex', 'hid')), may hold values from 0 to 15, all different within a row; in each aligned block of 16 rows (0 to 15, 16 to 31, ...) at most 8 rows name the same one
- w_gate: bfloat16 [32, 704, 2048], P(('ex', 'hid')), may hold values from -0.125 to 0.125
- w_up: bfloat16 [32, 704, 2048], P(('ex', 'hid')), may hold values from -0.125 to 0.125
- w_down: bfloat16 [32, 704, 2048], P(('ex', 'hid')), may hold values from -0.15625 to 0.15625
Outputs:
- grad_tokens: bfloat16 [512, 2048], P(('ex', 'hid'))
The draws below stay inside these ranges and needn't reach their ends.
Inputs may be any that keep to these rules, and one draw needn't show every extreme that they name: `routes`: among the 16 tokens of one device (aligned blocks of rows) no expert is named more than 8 times, a bound that some block reaches; a token's 4 experts differ.
All inputs are finite; a program needn't handle non-finite values.
Results may differ from the reference program's by a relative error of at most 0.007.
Values may be sent and summed in bfloat16 or wider, within the bound.
A program may use at most 64 MiB of HBM per device.

```python
import math
import jax
import jax.numpy as jnp
import numpy as np
from jax import lax

D = 2048
FF = 1408
TOP = 4
TOK_DEV = 16
EXPERTS = 16
BLOCKS = 2
TOKENS = 512
SLOT = 8
CAP = 256
N_EX = 8
N_HID = 4


def level_of(key, extent, cuts, least, high):
    factor_of, own = 1.0, jax.random.fold_in(key, 6)
    for axis_at, parts in cuts:
        steps = jnp.exp(jax.random.uniform(jax.random.fold_in(own, axis_at), (parts,), jnp.float32, least / len(cuts), high / len(cuts)))
        factor_of = factor_of * jnp.repeat(steps, extent[axis_at] // parts).reshape([-1 if axis == axis_at else 1 for axis in range(len(extent))])
    return factor_of


def assign_block(key, own, number, rows, number_of, top, reach, skew):
    ranking = jax.random.permutation(key, number_of)
    heavy_load, usual = portions_of(number_of, rows * top, reach, skew, True), portions_of(number_of, rows * top, reach, skew, False)
    places = jnp.arange(number_of)

    def named(tallies, rotation):
        used = int((tallies > 0).sum())
        fixed = max(1, used // 4)
        moved = fixed + (places - fixed + rotation * (used - fixed)) % max(1, number_of - fixed)
        return jnp.zeros((number_of,), jnp.int32).at[ranking[jnp.where(places < fixed, places, moved)]].set(jnp.asarray(tallies, jnp.int32))

    tallies = jnp.where(number % 4 == 0, named(heavy_load, number // 4), named(usual, number - number // 4 - 1))
    mixed = jax.random.permutation(jax.random.fold_in(own, 3), number_of)
    giver, sink = mixed[0:number_of // 2 * 2:2], mixed[1:number_of // 2 * 2:2]
    margin = jnp.minimum(tallies[giver] - 1, reach - tallies[sink]) // 2
    margin = jnp.where((giver == ranking[0]) | (sink == ranking[0]) | (tallies[sink] == 0), 0, jnp.maximum(margin, 0))
    moved = jax.random.randint(jax.random.fold_in(own, 4), (number_of // 2,), 0, 1 << 20) % (margin + 1)
    tallies = tallies.at[giver].add(-moved).at[sink].add(moved)
    items = jnp.searchsorted(jnp.cumsum(tallies), jnp.arange(rows * top), side="right").astype(jnp.int32)
    table = items.reshape(top, rows).T
    table = table[jax.random.permutation(jax.random.fold_in(own, 1), rows)]
    rotation = jax.random.randint(jax.random.fold_in(own, 2), (rows, 1), 0, top)
    return jnp.take_along_axis(table, (jnp.arange(top)[None, :] + rotation) % top, axis=1)


def portions_of(count, total, most, slope, full):
    weights = [(1 << 20) // math.isqrt(rank ** slope) + 1 for rank in range(1, count + 1)]
    largest = most if full else min(most, max(-(-total // count), total * weights[0] // sum(weights)))
    least = 1 if total - largest >= count - 1 else 0
    given, surplus = [largest] + [least] * (count - 1), total - largest - least * (count - 1)
    while surplus > 0:
        candidates = [i for i in range(1, count) if given[i] < largest] or [i for i in range(1, count) if given[i] < most]
        pool, budget = sum([weights[i] for i in candidates]), surplus
        for i in candidates:
            more = min(most - given[i], max(1, budget * weights[i] // pool), surplus)
            given[i] = given[i] + more
            surplus = surplus - more
    return np.array(given)


def normal_values(own_key, shape, scale, reach, split=(), kind=jnp.bfloat16):
    gain = level_of(own_key, shape, split, -0.22, 0.18) if split else 1.0
    entries = jax.random.normal(own_key, shape, jnp.float32) * scale * gain
    return jnp.minimum(jnp.maximum(entries, -reach), reach).astype(kind)


def setup_inputs(seed: int = 0) -> dict:
    streams_of = jax.random.split(jax.random.key(seed), 8)
    tokens = normal_values(streams_of[0], (TOKENS, D), 1.0, 6.0, ((0, 32),))
    cotangent = normal_values(streams_of[1], (TOKENS, D), 1.0, 6.0, ((0, 32),))
    gates = jnp.clip(jnp.exp(math.log(1.0) - 2.3025851 * jax.random.uniform(streams_of[2], (TOKENS, TOP), jnp.float32) ** level_of(streams_of[2], (TOKENS, TOP), ((0, 32),), -0.2, 0.2)), 0.1, 1.0)
    routes_keys = jax.random.split(jax.random.fold_in(streams_of[3], 1), TOKENS // TOK_DEV)
    routes_turns = jax.random.permutation(jax.random.fold_in(streams_of[3], 3), TOKENS // TOK_DEV)
    routes = jax.vmap(lambda own, number: assign_block(jax.random.fold_in(streams_of[3], 2), own, number, TOK_DEV, EXPERTS, TOP, SLOT, 2))(routes_keys, routes_turns).reshape((TOKENS, TOP))
    w_gate = normal_values(streams_of[4], (EXPERTS * BLOCKS, FF // BLOCKS, D), D ** -0.5, 0.125, ((0, 32),))
    w_up = normal_values(streams_of[5], (EXPERTS * BLOCKS, FF // BLOCKS, D), D ** -0.5, 0.125, ((0, 32),))
    w_down = normal_values(streams_of[6], (EXPERTS * BLOCKS, FF // BLOCKS, D), FF ** -0.5, 0.15625, ((0, 32),))
    return {"tokens": tokens, "cotangent": cotangent, "gates": gates, "routes": routes, "w_gate": w_gate, "w_up": w_up, "w_down": w_down}


def slots_of(flat):
    count = flat.shape[1]
    same = flat[:, :, None] == flat[:, None, :]
    order = jnp.arange(count, dtype=jnp.int32)
    earlier = order[None, :] < order[:, None]
    return lax.optimization_barrier(jnp.sum(jnp.where(same & earlier[None], 1, 0), axis=2)).astype(jnp.int32)

def hidden_grad(inputs, cotan, wgate, wup, wdown):
    dims = (((1,), (1,)), ((), ()))
    gate = lax.dot_general(inputs, wgate, dims, preferred_element_type=jnp.float32)
    upper = lax.dot_general(inputs, wup, dims, preferred_element_type=jnp.float32)
    hidden = lax.dot_general(cotan, wdown, dims, preferred_element_type=jnp.float32)
    sig = jax.nn.sigmoid(gate)
    d_up = (hidden * gate * sig).astype(jnp.bfloat16)
    d_gate = (hidden * upper * sig * (1.0 + gate * (1.0 - sig))).astype(jnp.bfloat16)
    first = jnp.dot(d_gate, wgate, preferred_element_type=jnp.float32)
    second = jnp.dot(d_up, wup, preferred_element_type=jnp.float32)
    return first + second

def reference(tokens, cotangent, gates, routes, w_gate, w_up, w_down):
    devices = N_EX * N_HID
    flat = routes.reshape(devices, TOK_DEV * TOP)
    slot = slots_of(flat)
    device = jnp.arange(devices, dtype=jnp.int32)[:, None]
    source = device // N_HID
    within = device % N_HID
    place = ((within * N_EX + source) * SLOT + slot).reshape(-1).astype(jnp.int32)
    expert_of = routes.reshape(-1)
    assign = jnp.arange(TOKENS * TOP, dtype=jnp.int32)
    x_pad = jnp.concatenate([tokens, jnp.zeros((1, D), jnp.bfloat16)], axis=0)
    dy_pad = jnp.concatenate([cotangent, jnp.zeros((1, D), jnp.bfloat16)], axis=0)
    gate_pad = jnp.concatenate([gates.reshape(-1), jnp.zeros((1,), jnp.float32)])
    width = FF // BLOCKS
    full_gate = w_gate.reshape(EXPERTS, FF, D)
    full_up = w_up.reshape(EXPERTS, FF, D)
    full_down = w_down.reshape(EXPERTS, FF, D)

    def one(acc, inputs):
        wgate, wup, wdown, expert = inputs
        target = jnp.where(expert_of == expert, place, CAP).astype(jnp.int32)
        inverse = jnp.full((CAP,), TOKENS * TOP, jnp.int32).at[target].set(assign, mode='drop')
        owner = inverse // TOP
        rows_x = x_pad[owner]
        rows_dy = (gate_pad[inverse][:, None] * dy_pad[owner].astype(jnp.float32)).astype(jnp.bfloat16)
        total = jnp.zeros((CAP, D), jnp.float32)
        for block in range(BLOCKS):
            lo = block * width
            term = hidden_grad(rows_x, rows_dy, wgate[lo:lo + width, :], wup[lo:lo + width, :], wdown[lo:lo + width, :])
            total = total + lax.optimization_barrier(term.astype(jnp.bfloat16)).astype(jnp.float32)
        result = lax.optimization_barrier(total.astype(jnp.bfloat16)).astype(jnp.float32)
        return (acc.at[owner].add(result), None)
    start = jnp.zeros((TOKENS + 1, D), jnp.float32)
    experts = jnp.arange(EXPERTS, dtype=jnp.int32)
    acc, unused = lax.scan(one, start, (full_gate, full_up, full_down, experts))
    return acc[:TOKENS].astype(jnp.bfloat16)
```

```python
import functools

import jax
import jax.numpy as jnp
from jax import lax
from jax.experimental import pallas as pl
from jax.experimental.pallas import tpu as pltpu
from jax.sharding import PartitionSpec as P

EXP_DEV = 2
CORES = 2
LANES = 128
F32 = jnp.float32
BF16 = jnp.bfloat16


def dense_kernel(
    blocks, tok_ref, cot_ref, gates_ref, routes_ref, wg_hbm, wu_hbm, wd_hbm, out_ref,
    rows, wg, wu, wd, ys, dgs, dus, part, from_sib, pair, from_x, from_y, half_x, half_y,
    from_y2, from_x2, plane, from_z, w_sem, send_sem, recv_sem,
):
    tok_dev, width = tok_ref.shape
    top = gates_ref.shape[1]
    half = width // 2
    ex, hid = lax.axis_index("ex"), lax.axis_index("hid")
    z, c = ex // CORES, ex % CORES
    y, x = hid // 2, hid % 2
    expert = (ex * lax.axis_size("hid") + hid) // blocks
    experts = EXP_DEV * lax.axis_size("ex")

    loads = [
        pltpu.make_async_copy(src.at[0], dst, w_sem.at[i])
        for i, (src, dst) in enumerate(((wg_hbm, wg), (wu_hbm, wu), (wd_hbm, wd)))
    ]
    for load in loads:
        load.start()

    def device(zz, cc, yy, xx):
        return (zz * CORES + cc, yy * 2 + xx)

    z_of = (z, z + 1 - 2 * (z % 2), (z + 2) % 4, 3 - z)
    at_x = device(z, c, y, 1 - x)
    at_y = device(z, c, 1 - y, x)
    sibling = device(z, 1 - c, y, x)
    at_z = [device(zz, c, y, x) for zz in z_of]
    partners = [at_x, at_y, sibling] + at_z[1:]
    barrier = pltpu.get_barrier_semaphore()
    for partner in partners:
        pl.semaphore_signal(barrier, inc=1, device_id=partner, device_id_type=pl.DeviceIdType.MESH)

    lane = lax.broadcasted_iota(jnp.int32, (tok_dev, LANES), 1)
    dense = jnp.zeros((tok_dev, LANES), F32)
    for k in range(top):
        dense += jnp.where(lane % experts == routes_ref[:, k : k + 1], gates_ref[:, k : k + 1], 0.0)
    high = dense.astype(BF16).astype(F32)
    rest = dense - high
    mid = rest.astype(BF16).astype(F32)
    low = rest - mid
    term = lane // experts
    terms = jnp.where(term == 0, high, jnp.where(term == 1, mid, jnp.where(term == 2, low, 0.0)))
    rows[0, 0, 0, :tok_dev, :width] = tok_ref[...]
    rows[0, 0, 0, :tok_dev, width:] = terms.astype(BF16)
    rows[0, 0, 0, tok_dev:, :width] = cot_ref[...]
    rows[0, 0, 0, tok_dev:, width:] = jnp.zeros((tok_dev, LANES), BF16)
    pl.semaphore_wait(barrier, len(partners))

    copies = []

    def send(src, dst, target):
        k = len(copies)
        copy = pltpu.make_async_remote_copy(
            src_ref=src, dst_ref=dst, send_sem=send_sem.at[k], recv_sem=recv_sem.at[k],
            device_id=target, device_id_type=pl.DeviceIdType.MESH,
        )
        copy.start()
        copies.append(copy)
        return copy

    along_z, along_x, along_y, diag_x, diag_y, cross = [None] * 4, [None] * 4, [None] * 4, [None] * 4, [None] * 4, {}

    def spread(i):
        along_x[i] = send(rows.at[i, 0, 0], rows.at[i, 0, 1], at_x)
        along_y[i] = send(rows.at[i, 0, 0], rows.at[i, 0, 2], at_y)
        cross[i, 0] = send(rows.at[i, 0, 0], rows.at[i, 1, 0], sibling)

    def relay(i):
        along_x[i].wait_recv()
        diag_y[i] = send(rows.at[i, 0, 1, pl.ds(0, tok_dev)], rows.at[i, 0, 3, pl.ds(0, tok_dev)], at_y)
        cross[i, 1] = send(rows.at[i, 0, 1], rows.at[i, 1, 1], sibling)
        along_y[i].wait_recv()
        diag_x[i] = send(
            rows.at[i, 0, 2, pl.ds(tok_dev, tok_dev)], rows.at[i, 0, 3, pl.ds(tok_dev, tok_dev)], at_x
        )
        cross[i, 2] = send(rows.at[i, 0, 2], rows.at[i, 1, 2], sibling)

    def close(i):
        diag_y[i].wait_recv()
        diag_x[i].wait_recv()
        cross[i, 3] = send(rows.at[i, 0, 3], rows.at[i, 1, 3], sibling)

    def arrived(i):
        for r in range(4):
            cross[i, r].wait_recv()

    def expand(i):
        count = 2 * CORES * 4 * tok_dev
        gate_rows = rows[pl.ds(i, 2), :, :, pl.ds(0, tok_dev), pl.ds(width, LANES)].reshape(count, LANES)
        lanes = lax.broadcasted_iota(jnp.int32, (count, LANES), 1)
        mine = (lanes % experts == expert) & (lanes < 3 * experts)
        gate = jnp.sum(jnp.where(mine, gate_rows.astype(F32), 0.0), axis=1, keepdims=True)
        cot = rows[pl.ds(i, 2), :, :, pl.ds(tok_dev, tok_dev), pl.ds(0, width)].reshape(count, width)
        ys[...] = (gate * cot.astype(F32)).astype(BF16)

    def hidden(i):
        count = 2 * CORES * 4 * tok_dev
        dims = (((1,), (1,)), ((), ()))
        inputs = rows[pl.ds(i, 2), :, :, pl.ds(0, tok_dev), pl.ds(0, width)].reshape(count, width)
        gate = lax.dot_general(inputs, wg[...], dims, preferred_element_type=F32)
        upper = lax.dot_general(inputs, wu[...], dims, preferred_element_type=F32)
        down = lax.dot_general(ys[...], wd[...], dims, preferred_element_type=F32)
        sig = jax.nn.sigmoid(gate)
        dus[...] = (down * gate * sig).astype(BF16)
        dgs[...] = (down * upper * sig * (1.0 + gate * (1.0 - sig))).astype(BF16)

    def back(i):
        step = width // 4

        def body(n, carry):
            at = pl.ds(pl.multiple_of(n * step, step), step)
            value = jnp.dot(dgs[...], wg[:, at], preferred_element_type=F32)
            value += jnp.dot(dus[...], wu[:, at], preferred_element_type=F32)
            part[pl.ds(i, 2), :, :, :, at] = value.astype(BF16).reshape(2, CORES, 4, tok_dev, step)
            return carry

        lax.fori_loop(0, 4, body, 0)

    sib, first_x, first_y, second_x, second_y, home = {}, {}, {}, {}, {}, {}

    def reduce_sibling(i):
        sib[i] = send(part.at[i, 1], from_sib.at[i], sibling)

    def reduce_first(i):
        sib[i].wait_recv()
        total = part[i, 0].astype(F32) + from_sib[i].astype(F32)
        pair[i] = total.astype(BF16).reshape(2, 2, tok_dev, width)
        first_x[i] = send(pair.at[i, :, 1, :, pl.ds(0, half)], from_x.at[i], at_x)
        first_y[i] = send(pair.at[i, 1, :, :, pl.ds(half, half)], from_y.at[i], at_y)

    def reduce_second(i):
        first_x[i].wait_recv()
        half_x[i] = (pair[i, :, 0, :, :half].astype(F32) + from_x[i].astype(F32)).astype(BF16)
        second_y[i] = send(half_x.at[i, 1], from_y2.at[i], at_y)
        first_y[i].wait_recv()
        half_y[i] = (pair[i, 0, :, :, half:].astype(F32) + from_y[i].astype(F32)).astype(BF16)
        second_x[i] = send(half_y.at[i, 1], from_x2.at[i], at_x)

    def reduce_third(i):
        second_y[i].wait_recv()
        second_x[i].wait_recv()
        left = half_x[i, 0].astype(F32) + from_y2[i].astype(F32)
        right = half_y[i, 0].astype(F32) + from_x2[i].astype(F32)
        plane[i, :, :half] = left.astype(BF16)
        plane[i, :, half:] = right.astype(BF16)
        if i:
            home[i] = send(plane.at[i], from_z.at[i - 1], at_z[i])

    spread(0)
    for i in (1, 2, 3):
        along_z[i] = send(rows.at[0, 0, 0], rows.at[i, 0, 0], at_z[i])
    for i in (1, 2, 3):
        along_z[i].wait_recv()
        spread(i)
        relay(i - 1)
        if i > 1:
            close(i - 2)
    for load in loads:
        load.wait()
    arrived(0)
    relay(3)
    close(2)
    arrived(1)
    expand(0)
    close(3)
    hidden(0)
    back(0)
    reduce_sibling(0)
    reduce_sibling(1)
    arrived(2)
    arrived(3)
    expand(2)
    reduce_first(1)
    reduce_first(0)
    hidden(2)
    reduce_second(1)
    reduce_second(0)
    back(2)
    reduce_sibling(2)
    reduce_sibling(3)
    reduce_third(1)
    reduce_third(0)
    for i in (2, 3):
        reduce_first(i)
    for i in (2, 3):
        reduce_second(i)
    for i in (2, 3):
        reduce_third(i)

    total = plane[0].astype(F32)
    for i in (1, 2, 3):
        home[i].wait_recv()
        total += from_z[i - 1].astype(F32)
    out_ref[...] = total.astype(BF16)
    for copy in copies:
        copy.wait_send()


def dense(tokens, cotangent, gates, routes, w_gate, w_up, w_down):
    tok_dev, width = tokens.shape
    units = w_gate.shape[1]
    blocks = lax.axis_size("hid") // EXP_DEV
    count = 2 * CORES * 4 * tok_dev
    half = width // 2
    vmem, anywhere = pl.BlockSpec(memory_space=pltpu.VMEM), pl.BlockSpec(memory_space=pl.ANY)
    copies = 58
    return pl.pallas_call(
        functools.partial(dense_kernel, blocks),
        out_shape=jax.ShapeDtypeStruct((tok_dev, width), BF16),
        in_specs=[vmem] * 4 + [anywhere] * 3,
        out_specs=vmem,
        scratch_shapes=[
            pltpu.VMEM((4, CORES, 4, 2 * tok_dev, width + LANES), BF16),
            pltpu.VMEM((units, width), BF16),
            pltpu.VMEM((units, width), BF16),
            pltpu.VMEM((units, width), BF16),
            pltpu.VMEM((count, width), BF16),
            pltpu.VMEM((count, units), BF16),
            pltpu.VMEM((count, units), BF16),
            pltpu.VMEM((4, CORES, 4, tok_dev, width), BF16),
            pltpu.VMEM((4, 4, tok_dev, width), BF16),
            pltpu.VMEM((4, 2, 2, tok_dev, width), BF16),
            pltpu.VMEM((4, 2, tok_dev, half), BF16),
            pltpu.VMEM((4, 2, tok_dev, half), BF16),
            pltpu.VMEM((4, 2, tok_dev, half), BF16),
            pltpu.VMEM((4, 2, tok_dev, half), BF16),
            pltpu.VMEM((4, tok_dev, half), BF16),
            pltpu.VMEM((4, tok_dev, half), BF16),
            pltpu.VMEM((4, tok_dev, width), BF16),
            pltpu.VMEM((3, tok_dev, width), BF16),
            pltpu.SemaphoreType.DMA((3,)),
            pltpu.SemaphoreType.DMA((copies,)),
            pltpu.SemaphoreType.DMA((copies,)),
        ],
        compiler_params=pltpu.CompilerParams(
            collective_id=0, has_side_effects=True, vmem_limit_bytes=50 * 1024 * 1024
        ),
    )(tokens, cotangent, gates, routes, w_gate, w_up, w_down)


def hidden_grad(inputs, cotan, wgate, wup, wdown):
    dims = (((1,), (1,)), ((), ()))
    gate = lax.dot_general(inputs, wgate, dims, preferred_element_type=jnp.float32)
    upper = lax.dot_general(inputs, wup, dims, preferred_element_type=jnp.float32)
    hidden = lax.dot_general(cotan, wdown, dims, preferred_element_type=jnp.float32)
    sig = jax.nn.sigmoid(gate)
    d_up = (hidden * gate * sig).astype(jnp.bfloat16)
    d_gate = (hidden * upper * sig * (1.0 + gate * (1.0 - sig))).astype(jnp.bfloat16)
    first = jnp.dot(d_gate, wgate, preferred_element_type=jnp.float32)
    second = jnp.dot(d_up, wup, preferred_element_type=jnp.float32)
    return first + second


def per_device(tokens, cotangent, gates, routes, w_gate, w_up, w_down):
    n_ex = lax.axis_size("ex")
    n_hid = lax.axis_size("hid")
    tok_dev, width = tokens.shape
    top = routes.shape[1]
    experts_all = EXP_DEV * n_ex
    blocks = n_hid // EXP_DEV
    slot_cap = max(2, (2 * tok_dev * top + experts_all - 1) // experts_all)
    flat = routes.reshape(-1)
    count = flat.shape[0]
    order = jnp.arange(count, dtype=jnp.int32)
    same = flat[:, None] == flat[None, :]
    earlier = order[None, :] < order[:, None]
    slot = jnp.sum(jnp.where(same & earlier, 1, 0), axis=1).astype(jnp.int32)
    owner_ex = flat // EXP_DEV
    local = flat % EXP_DEV
    rows_x = jnp.repeat(tokens, top, axis=0)
    rows_dy = jnp.repeat(cotangent, top, axis=0).astype(jnp.float32)
    scaled = (gates.reshape(-1)[:, None] * rows_dy).astype(jnp.bfloat16)
    stacked = jnp.stack([rows_x, scaled], axis=1)
    buffer = (
        jnp.zeros((EXP_DEV, 2, n_ex, slot_cap, width), jnp.bfloat16)
        .at[local, :, owner_ex, slot]
        .set(stacked)
    )
    arrived = lax.all_to_all(buffer, "ex", split_axis=2, concat_axis=2, tiled=True)
    tail = arrived.shape[1:]
    received = lax.all_to_all(
        jnp.broadcast_to(arrived[:, None], (EXP_DEV, blocks) + tail).reshape((n_hid,) + tail),
        "hid",
        split_axis=0,
        concat_axis=0,
        tiled=True,
    )
    rows = n_hid * n_ex * slot_cap
    inputs = received[:, 0].reshape(rows, width)
    cotan = received[:, 1].reshape(rows, width)
    partial_value = hidden_grad(inputs, cotan, w_gate[0], w_up[0], w_down[0]).astype(jnp.bfloat16)
    partial_value = partial_value.reshape(n_hid, n_ex, slot_cap, width)
    moved = lax.all_to_all(partial_value, "ex", split_axis=1, concat_axis=1, tiled=True)
    landed = lax.all_to_all(moved, "hid", split_axis=0, concat_axis=0, tiled=True)
    back = jnp.sum(
        landed.astype(jnp.float32).reshape(EXP_DEV, blocks, n_ex, slot_cap, width), axis=1
    ).astype(jnp.bfloat16)
    index = (local * n_ex + owner_ex) * slot_cap + slot
    picked = back.reshape(-1, width)[index].reshape(tok_dev, top, width).astype(jnp.float32)
    return jnp.sum(picked, axis=1).astype(jnp.bfloat16)


def solution(mesh):
    in_specs = (
        P(("ex", "hid"), None),
        P(("ex", "hid"), None),
        P(("ex", "hid"), None),
        P(("ex", "hid"), None),
        P(("ex", "hid"), None, None),
        P(("ex", "hid"), None, None),
        P(("ex", "hid"), None, None),
    )
    out_specs = P(("ex", "hid"), None)
    small = mesh.shape["ex"] == 4 * CORES and mesh.shape["hid"] == 4
    return jax.shard_map(
        dense if small else per_device, mesh=mesh, in_specs=in_specs, out_specs=out_specs, check_vma=False
    )
```

```python
import functools

import jax
import jax.numpy as jnp
from jax import lax
from jax.experimental import pallas as pl
from jax.experimental.pallas import tpu as pltpu
from jax.sharding import PartitionSpec as P

EXP_DEV = 2
CORES = 2
LANES = 128
F32 = jnp.float32
BF16 = jnp.bfloat16


def dense_kernel(
    blocks, tok_ref, cot_ref, gates_ref, routes_ref, wg_hbm, wu_hbm, wd_hbm, out_ref,
    rows, small_g, small_r, wg, wu, wd, xs, ys, gt, ut, dgs, dus, part, from_sib, pair, from_x, from_y,
    half_x, half_y, from_y2, from_x2, plane, from_z, result, in_sem, w_sem, send_sem, recv_sem,
):
    tok_dev, width = tok_ref.shape
    top = gates_ref.shape[0]
    half = width // 2
    ex, hid = lax.axis_index("ex"), lax.axis_index("hid")
    z, c = ex // CORES, ex % CORES
    y, x = hid // 2, hid % 2
    expert = (ex * lax.axis_size("hid") + hid) // blocks
    experts = EXP_DEV * lax.axis_size("ex")

    first = [
        pltpu.make_async_copy(src, dst, in_sem.at[i])
        for i, (src, dst) in enumerate(
            (
                (gates_ref, small_g),
                (routes_ref, small_r),
                (tok_ref, rows.at[0, 0, 0, pl.ds(0, tok_dev), pl.ds(0, width)]),
                (cot_ref, rows.at[0, 0, 0, pl.ds(tok_dev, tok_dev), pl.ds(0, width)]),
            )
        )
    ]
    for load in first:
        load.start()
    loads = [
        pltpu.make_async_copy(src.at[0], dst, w_sem.at[i])
        for i, (src, dst) in enumerate(((wg_hbm, wg), (wu_hbm, wu), (wd_hbm, wd)))
    ]
    for load in loads:
        load.start()

    def device(zz, cc, yy, xx):
        return (zz * CORES + cc, yy * 2 + xx)

    z_of = (z, z + 1 - 2 * (z % 2), (z + 2) % 4, 3 - z)
    at_x = device(z, c, y, 1 - x)
    at_y = device(z, c, 1 - y, x)
    sibling = device(z, 1 - c, y, x)
    at_z = [device(zz, c, y, x) for zz in z_of]
    partners = [at_x, at_y, sibling] + at_z[1:]
    barrier = pltpu.get_barrier_semaphore()
    for partner in partners:
        pl.semaphore_signal(barrier, inc=1, device_id=partner, device_id_type=pl.DeviceIdType.MESH)

    lane = lax.broadcasted_iota(jnp.int32, (tok_dev, LANES), 1)
    dense = jnp.zeros((tok_dev, LANES), F32)
    diagonal = lax.broadcasted_iota(jnp.int32, (tok_dev, tok_dev), 0) == lax.broadcasted_iota(
        jnp.int32, (tok_dev, tok_dev), 1
    )
    place = (lane % experts).astype(F32)
    first[0].wait()
    first[1].wait()
    for k in range(top):
        gate_k = jnp.sum(jnp.where(diagonal, small_g[k : k + 1, :], 0.0), axis=1, keepdims=True)
        route_k = jnp.sum(jnp.where(diagonal, small_r[k : k + 1, :].astype(F32), 0.0), axis=1, keepdims=True)
        dense += jnp.where(place == route_k, gate_k, 0.0)
    high = dense.astype(BF16).astype(F32)
    rest = dense - high
    mid = rest.astype(BF16).astype(F32)
    low = rest - mid
    term = lane // experts
    terms = jnp.where(term == 0, high, jnp.where(term == 1, mid, jnp.where(term == 2, low, 0.0)))
    rows[0, 0, 0, :tok_dev, width:] = terms.astype(BF16)
    rows[0, 0, 0, tok_dev:, width:] = jnp.zeros((tok_dev, LANES), BF16)
    first[2].wait()
    first[3].wait()
    pl.semaphore_wait(barrier, len(partners))

    copies = []

    def send(src, dst, target):
        k = len(copies)
        copy = pltpu.make_async_remote_copy(
            src_ref=src, dst_ref=dst, send_sem=send_sem.at[k], recv_sem=recv_sem.at[k],
            device_id=target, device_id_type=pl.DeviceIdType.MESH,
        )
        copy.start()
        copies.append(copy)
        return copy

    along_z, along_x, along_y, diag_x, diag_y, cross = [None] * 4, [None] * 4, [None] * 4, [None] * 4, [None] * 4, {}

    def spread(i):
        along_x[i] = send(rows.at[i, 0, 0], rows.at[i, 0, 1], at_x)
        along_y[i] = send(rows.at[i, 0, 0], rows.at[i, 0, 2], at_y)
        cross[i, 0] = send(rows.at[i, 0, 0], rows.at[i, 1, 0], sibling)

    def relay(i):
        along_x[i].wait_recv()
        diag_y[i] = send(rows.at[i, 0, 1, pl.ds(0, tok_dev)], rows.at[i, 0, 3, pl.ds(0, tok_dev)], at_y)
        cross[i, 1] = send(rows.at[i, 0, 1], rows.at[i, 1, 1], sibling)
        along_y[i].wait_recv()
        diag_x[i] = send(
            rows.at[i, 0, 2, pl.ds(tok_dev, tok_dev)], rows.at[i, 0, 3, pl.ds(tok_dev, tok_dev)], at_x
        )
        cross[i, 2] = send(rows.at[i, 0, 2], rows.at[i, 1, 2], sibling)

    def close(i):
        diag_y[i].wait_recv()
        diag_x[i].wait_recv()
        cross[i, 3] = send(rows.at[i, 0, 3], rows.at[i, 1, 3], sibling)

    def arrived(i):
        for r in range(4):
            cross[i, r].wait_recv()

    count = 2 * CORES * 4 * tok_dev
    units = wg.shape[0]
    rhs_last = (((1,), (1,)), ((), ()))

    def expand(i):
        gate_rows = rows[pl.ds(i, 2), :, :, pl.ds(0, tok_dev), pl.ds(width, LANES)].reshape(count, LANES)
        lanes = lax.broadcasted_iota(jnp.int32, (count, LANES), 1)
        mine = (lanes % experts == expert) & (lanes < 3 * experts)
        gate = jnp.sum(jnp.where(mine, gate_rows.astype(F32), 0.0), axis=1, keepdims=True)
        cot = rows[pl.ds(i, 2), :, :, pl.ds(tok_dev, tok_dev), pl.ds(0, width)].reshape(count, width)
        ys[...] = (gate * cot.astype(F32)).astype(BF16)
        xs[...] = rows[pl.ds(i, 2), :, :, pl.ds(0, tok_dev), pl.ds(0, width)].reshape(count, width)

    def product_gate():
        gt[...] = lax.dot_general(wg[...], xs[...], rhs_last, preferred_element_type=F32)

    def product_up():
        ut[...] = lax.dot_general(wu[...], xs[...], rhs_last, preferred_element_type=F32)

    def product_down():
        down = lax.dot_general(wd[...], ys[...], rhs_last, preferred_element_type=F32)
        gate = gt[...]
        sig = jax.nn.sigmoid(gate)
        dus[...] = (down * gate * sig).T.astype(BF16)
        dgs[...] = (down * ut[...] * sig * (1.0 + gate * (1.0 - sig))).T.astype(BF16)

    def back(i, which):
        step = half // 2

        def body(n, carry):
            at = pl.ds(pl.multiple_of(which * half + n * step, step), step)
            value = jnp.dot(dgs[...], wg[:, at], preferred_element_type=F32)
            value += jnp.dot(dus[...], wu[:, at], preferred_element_type=F32)
            part[pl.ds(i, 2), :, :, :, at] = value.astype(BF16).reshape(2, CORES, 4, tok_dev, step)
            return carry

        lax.fori_loop(0, 2, body, 0)
        for k in (i + 1, i):
            at = pl.ds(which * half, half)
            sib[k, which] = send(part.at[k, 1, :, :, at], from_sib.at[k, :, :, at], sibling)

    sib, first_x, first_y, second_x, second_y, home = {}, {}, {}, {}, {}, {}

    def reduce_first(i, which):
        sib[i, which].wait_recv()
        at = pl.ds(which * half, half)
        total = part[i, 0, :, :, at].astype(F32) + from_sib[i, :, :, at].astype(F32)
        pair[i, :, :, :, at] = total.astype(BF16).reshape(2, 2, tok_dev, half)
        if which == 0:
            first_x[i] = send(pair.at[i, :, 1, :, at], from_x.at[i], at_x)
        else:
            first_y[i] = send(pair.at[i, 1, :, :, at], from_y.at[i], at_y)

    def reduce_second(i):
        first_x[i].wait_recv()
        half_x[i] = (pair[i, :, 0, :, :half].astype(F32) + from_x[i].astype(F32)).astype(BF16)
        second_y[i] = send(half_x.at[i, 1], from_y2.at[i], at_y)
        first_y[i].wait_recv()
        half_y[i] = (pair[i, 0, :, :, half:].astype(F32) + from_y[i].astype(F32)).astype(BF16)
        second_x[i] = send(half_y.at[i, 1], from_x2.at[i], at_x)

    def reduce_third(i):
        second_y[i].wait_recv()
        second_x[i].wait_recv()
        left = half_x[i, 0].astype(F32) + from_y2[i].astype(F32)
        right = half_y[i, 0].astype(F32) + from_x2[i].astype(F32)
        plane[i, :, :half] = left.astype(BF16)
        plane[i, :, half:] = right.astype(BF16)
        if i:
            home[i] = send(plane.at[i], from_z.at[i - 1], at_z[i])

    spread(0)
    for i in (1, 2, 3):
        along_z[i] = send(rows.at[0, 0, 0], rows.at[i, 0, 0], at_z[i])
    for i in (1, 2):
        along_z[i].wait_recv()
        spread(i)
        relay(i - 1)
    close(0)
    along_z[3].wait_recv()
    spread(3)
    close(1)
    arrived(0)
    arrived(1)
    expand(0)
    for load in loads:
        load.wait()
    relay(2)
    product_gate()
    product_up()
    close(2)
    relay(3)
    product_down()
    close(3)
    back(0, 0)
    back(0, 1)
    for i in (1, 0):
        reduce_first(i, 0)
        reduce_first(i, 1)
    arrived(2)
    arrived(3)
    expand(2)
    product_gate()
    reduce_second(1)
    product_up()
    reduce_second(0)
    product_down()
    reduce_third(1)
    reduce_third(0)
    back(2, 0)
    back(2, 1)
    for which in (0, 1):
        reduce_first(3, which)
        reduce_first(2, which)
    for i in (3, 2):
        reduce_second(i)
    for i in (3, 2):
        reduce_third(i)
    total = plane[0].astype(F32)
    for i in (1, 2, 3):
        home[i].wait_recv()
        total += from_z[i - 1].astype(F32)
    result[...] = total.astype(BF16)
    store = pltpu.make_async_copy(result, out_ref, in_sem.at[0])
    store.start()
    for copy in copies:
        copy.wait_send()
    store.wait()


def dense(tokens, cotangent, gates, routes, w_gate, w_up, w_down):
    tok_dev, width = tokens.shape
    units = w_gate.shape[1]
    blocks = lax.axis_size("hid") // EXP_DEV
    count = 2 * CORES * 4 * tok_dev
    half = width // 2
    top = gates.shape[1]
    hbm = pl.BlockSpec(memory_space=pltpu.HBM)
    copies = 62
    return pl.pallas_call(
        functools.partial(dense_kernel, blocks),
        out_shape=jax.ShapeDtypeStruct((tok_dev, width), BF16),
        in_specs=[hbm] * 7,
        out_specs=hbm,
        scratch_shapes=[
            pltpu.VMEM((4, CORES, 4, 2 * tok_dev, width + LANES), BF16),
            pltpu.VMEM((top, tok_dev), F32),
            pltpu.VMEM((top, tok_dev), jnp.int32),
            pltpu.VMEM((units, width), BF16),
            pltpu.VMEM((units, width), BF16),
            pltpu.VMEM((units, width), BF16),
            pltpu.VMEM((count, width), BF16),
            pltpu.VMEM((count, width), BF16),
            pltpu.VMEM((units, count), F32),
            pltpu.VMEM((units, count), F32),
            pltpu.VMEM((count, units), BF16),
            pltpu.VMEM((count, units), BF16),
            pltpu.VMEM((4, CORES, 4, tok_dev, width), BF16),
            pltpu.VMEM((4, 4, tok_dev, width), BF16),
            pltpu.VMEM((4, 2, 2, tok_dev, width), BF16),
            pltpu.VMEM((4, 2, tok_dev, half), BF16),
            pltpu.VMEM((4, 2, tok_dev, half), BF16),
            pltpu.VMEM((4, 2, tok_dev, half), BF16),
            pltpu.VMEM((4, 2, tok_dev, half), BF16),
            pltpu.VMEM((4, tok_dev, half), BF16),
            pltpu.VMEM((4, tok_dev, half), BF16),
            pltpu.VMEM((4, tok_dev, width), BF16),
            pltpu.VMEM((3, tok_dev, width), BF16),
            pltpu.VMEM((tok_dev, width), BF16),
            pltpu.SemaphoreType.DMA((4,)),
            pltpu.SemaphoreType.DMA((3,)),
            pltpu.SemaphoreType.DMA((copies,)),
            pltpu.SemaphoreType.DMA((copies,)),
        ],
        compiler_params=pltpu.CompilerParams(
            collective_id=0, has_side_effects=True, vmem_limit_bytes=60 * 1024 * 1024
        ),
    )(tokens, cotangent, gates.T, routes.T, w_gate, w_up, w_down)


def hidden_grad(inputs, cotan, wgate, wup, wdown):
    dims = (((1,), (1,)), ((), ()))
    gate = lax.dot_general(inputs, wgate, dims, preferred_element_type=jnp.float32)
    upper = lax.dot_general(inputs, wup, dims, preferred_element_type=jnp.float32)
    hidden = lax.dot_general(cotan, wdown, dims, preferred_element_type=jnp.float32)
    sig = jax.nn.sigmoid(gate)
    d_up = (hidden * gate * sig).astype(jnp.bfloat16)
    d_gate = (hidden * upper * sig * (1.0 + gate * (1.0 - sig))).astype(jnp.bfloat16)
    first = jnp.dot(d_gate, wgate, preferred_element_type=jnp.float32)
    second = jnp.dot(d_up, wup, preferred_element_type=jnp.float32)
    return first + second


def per_device(tokens, cotangent, gates, routes, w_gate, w_up, w_down):
    n_ex = lax.axis_size("ex")
    n_hid = lax.axis_size("hid")
    tok_dev, width = tokens.shape
    top = routes.shape[1]
    experts_all = EXP_DEV * n_ex
    blocks = n_hid // EXP_DEV
    slot_cap = max(2, (2 * tok_dev * top + experts_all - 1) // experts_all)
    flat = routes.reshape(-1)
    count = flat.shape[0]
    order = jnp.arange(count, dtype=jnp.int32)
    same = flat[:, None] == flat[None, :]
    earlier = order[None, :] < order[:, None]
    slot = jnp.sum(jnp.where(same & earlier, 1, 0), axis=1).astype(jnp.int32)
    owner_ex = flat // EXP_DEV
    local = flat % EXP_DEV
    rows_x = jnp.repeat(tokens, top, axis=0)
    rows_dy = jnp.repeat(cotangent, top, axis=0).astype(jnp.float32)
    scaled = (gates.reshape(-1)[:, None] * rows_dy).astype(jnp.bfloat16)
    stacked = jnp.stack([rows_x, scaled], axis=1)
    buffer = (
        jnp.zeros((EXP_DEV, 2, n_ex, slot_cap, width), jnp.bfloat16)
        .at[local, :, owner_ex, slot]
        .set(stacked)
    )
    arrived = lax.all_to_all(buffer, "ex", split_axis=2, concat_axis=2, tiled=True)
    tail = arrived.shape[1:]
    received = lax.all_to_all(
        jnp.broadcast_to(arrived[:, None], (EXP_DEV, blocks) + tail).reshape((n_hid,) + tail),
        "hid",
        split_axis=0,
        concat_axis=0,
        tiled=True,
    )
    rows = n_hid * n_ex * slot_cap
    inputs = received[:, 0].reshape(rows, width)
    cotan = received[:, 1].reshape(rows, width)
    partial_value = hidden_grad(inputs, cotan, w_gate[0], w_up[0], w_down[0]).astype(jnp.bfloat16)
    partial_value = partial_value.reshape(n_hid, n_ex, slot_cap, width)
    moved = lax.all_to_all(partial_value, "ex", split_axis=1, concat_axis=1, tiled=True)
    landed = lax.all_to_all(moved, "hid", split_axis=0, concat_axis=0, tiled=True)
    back = jnp.sum(
        landed.astype(jnp.float32).reshape(EXP_DEV, blocks, n_ex, slot_cap, width), axis=1
    ).astype(jnp.bfloat16)
    index = (local * n_ex + owner_ex) * slot_cap + slot
    picked = back.reshape(-1, width)[index].reshape(tok_dev, top, width).astype(jnp.float32)
    return jnp.sum(picked, axis=1).astype(jnp.bfloat16)


def solution(mesh):
    in_specs = (
        P(("ex", "hid"), None),
        P(("ex", "hid"), None),
        P(("ex", "hid"), None),
        P(("ex", "hid"), None),
        P(("ex", "hid"), None, None),
        P(("ex", "hid"), None, None),
        P(("ex", "hid"), None, None),
    )
    out_specs = P(("ex", "hid"), None)
    small = mesh.shape["ex"] == 4 * CORES and mesh.shape["hid"] == 4
    return jax.shard_map(
        dense if small else per_device, mesh=mesh, in_specs=in_specs, out_specs=out_specs, check_vma=False
    )
```

```python
import functools

import jax
import jax.numpy as jnp
from jax import lax
from jax.experimental import pallas as pl
from jax.experimental.pallas import tpu as pltpu
from jax.sharding import PartitionSpec as P

EXP_DEV = 2
CORES = 2
LANES = 128
TILE = 256
F32 = jnp.float32
BF16 = jnp.bfloat16


def dense_kernel(
    blocks, tok_ref, cot_ref, gates_ref, routes_ref, wg_hbm, wu_hbm, wd_hbm, out_ref,
    rows, small_g, small_r, wg, wu, wd, xs, ys, dgs, dus, part, from_sib, pair, from_x, from_y,
    half_x, half_y, from_y2, from_x2, plane, from_z, in_sem, w_sem, send_sem, recv_sem,
):
    tok_dev, width = tok_ref.shape
    top = gates_ref.shape[0]
    units = wg_hbm.shape[1]
    half = width // 2
    ex, hid = lax.axis_index("ex"), lax.axis_index("hid")
    z, c = ex // CORES, ex % CORES
    y, x = hid // 2, hid % 2
    expert = (ex * lax.axis_size("hid") + hid) // blocks
    experts = EXP_DEV * lax.axis_size("ex")

    first = [
        pltpu.make_async_copy(src, dst, in_sem.at[i])
        for i, (src, dst) in enumerate(
            (
                (gates_ref, small_g),
                (routes_ref, small_r),
                (tok_ref, rows.at[0, 0, 0, :, pl.ds(0, width)]),
                (cot_ref, rows.at[0, 0, 0, :, pl.ds(width, width)]),
            )
        )
    ]
    for load in first:
        load.start()
    loads = [
        pltpu.make_async_copy(src.at[0], dst.at[pl.ds(0, units)], w_sem.at[i])
        for i, (src, dst) in enumerate(((wg_hbm, wg), (wu_hbm, wu), (wd_hbm, wd)))
    ]
    for load in loads:
        load.start()
    padded = wg.shape[0]
    for weight in (wg, wu, wd):
        weight[units:] = jnp.zeros((padded - units, width), BF16)

    def device(zz, cc, yy, xx):
        return (zz * CORES + cc, yy * 2 + xx)

    z_of = (z, z + 1 - 2 * (z % 2), (z + 2) % 4, 3 - z)
    at_x = device(z, c, y, 1 - x)
    at_y = device(z, c, 1 - y, x)
    sibling = device(z, 1 - c, y, x)
    at_z = [device(zz, c, y, x) for zz in z_of]
    partners = [at_x, at_y, sibling] + at_z[1:]
    barrier = pltpu.get_barrier_semaphore()
    for partner in partners:
        pl.semaphore_signal(barrier, inc=1, device_id=partner, device_id_type=pl.DeviceIdType.MESH)

    lane = lax.broadcasted_iota(jnp.int32, (tok_dev, LANES), 1)
    dense = jnp.zeros((tok_dev, LANES), F32)
    diagonal = lax.broadcasted_iota(jnp.int32, (tok_dev, tok_dev), 0) == lax.broadcasted_iota(
        jnp.int32, (tok_dev, tok_dev), 1
    )
    place = (lane % experts).astype(F32)
    first[0].wait()
    first[1].wait()
    for k in range(top):
        gate_k = jnp.sum(jnp.where(diagonal, small_g[k : k + 1, :], 0.0), axis=1, keepdims=True)
        route_k = jnp.sum(jnp.where(diagonal, small_r[k : k + 1, :].astype(F32), 0.0), axis=1, keepdims=True)
        dense += jnp.where(place == route_k, gate_k, 0.0)
    high = dense.astype(BF16).astype(F32)
    rest = dense - high
    mid = rest.astype(BF16).astype(F32)
    low = rest - mid
    term = lane // experts
    terms = jnp.where(term == 0, high, jnp.where(term == 1, mid, jnp.where(term == 2, low, 0.0)))
    rows[0, 0, 0, :, 2 * width :] = terms.astype(BF16)
    first[2].wait()
    first[3].wait()
    pl.semaphore_wait(barrier, len(partners))

    copies = []

    def send(src, dst, target):
        k = len(copies)
        copy = pltpu.make_async_remote_copy(
            src_ref=src, dst_ref=dst, send_sem=send_sem.at[k], recv_sem=recv_sem.at[k],
            device_id=target, device_id_type=pl.DeviceIdType.MESH,
        )
        copy.start()
        copies.append(copy)
        return copy

    along_z, along_x, along_y, diag_x, diag_y, cross = [None] * 4, [None] * 4, [None] * 4, [None] * 4, [None] * 4, {}

    def spread(i):
        along_x[i] = send(rows.at[i, 0, 0], rows.at[i, 0, 1], at_x)
        along_y[i] = send(rows.at[i, 0, 0], rows.at[i, 0, 2], at_y)
        cross[i, 0] = send(rows.at[i, 0, 0], rows.at[i, 1, 0], sibling)

    def relay(i):
        along_x[i].wait_recv()
        diag_y[i] = send(rows.at[i, 0, 1, :, pl.ds(0, width)], rows.at[i, 0, 3, :, pl.ds(0, width)], at_y)
        cross[i, 1] = send(rows.at[i, 0, 1], rows.at[i, 1, 1], sibling)
        along_y[i].wait_recv()
        diag_x[i] = send(
            rows.at[i, 0, 2, :, pl.ds(width, width + LANES)], rows.at[i, 0, 3, :, pl.ds(width, width + LANES)], at_x
        )
        cross[i, 2] = send(rows.at[i, 0, 2], rows.at[i, 1, 2], sibling)

    def close(i):
        diag_y[i].wait_recv()
        diag_x[i].wait_recv()
        cross[i, 3] = send(rows.at[i, 0, 3], rows.at[i, 1, 3], sibling)

    def arrived(i):
        for r in range(4):
            cross[i, r].wait_recv()

    count = 2 * CORES * 4 * tok_dev
    rhs_last = (((1,), (1,)), ((), ()))

    def expand(i):
        gate_rows = rows[pl.ds(i, 2), :, :, :, pl.ds(2 * width, LANES)].reshape(count, LANES)
        lanes = lax.broadcasted_iota(jnp.int32, (count, LANES), 1)
        mine = (lanes % experts == expert) & (lanes < 3 * experts)
        gate = jnp.sum(jnp.where(mine, gate_rows.astype(F32), 0.0), axis=1, keepdims=True)
        cot = rows[pl.ds(i, 2), :, :, :, pl.ds(width, width)].reshape(count, width)
        ys[...] = (gate * cot.astype(F32)).astype(BF16)
        xs[...] = rows[pl.ds(i, 2), :, :, :, pl.ds(0, width)].reshape(count, width)

    def forward():
        def body(n, carry):
            at = pl.ds(pl.multiple_of(n * TILE, TILE), TILE)
            gate = lax.dot_general(xs[...], wg[at, :], rhs_last, preferred_element_type=F32)
            upper = lax.dot_general(xs[...], wu[at, :], rhs_last, preferred_element_type=F32)
            down = lax.dot_general(ys[...], wd[at, :], rhs_last, preferred_element_type=F32)
            sig = jax.nn.sigmoid(gate)
            dus[:, at] = (down * gate * sig).astype(BF16)
            dgs[:, at] = (down * upper * sig * (1.0 + gate * (1.0 - sig))).astype(BF16)
            return carry

        lax.fori_loop(0, padded // TILE, body, 0)

    def back(i, which):
        step = half // 2

        def body(n, carry):
            at = pl.ds(pl.multiple_of(which * half + n * step, step), step)
            value = jnp.dot(dgs[...], wg[:, at], preferred_element_type=F32)
            value += jnp.dot(dus[...], wu[:, at], preferred_element_type=F32)
            part[pl.ds(i, 2), :, :, :, at] = value.astype(BF16).reshape(2, CORES, 4, tok_dev, step)
            return carry

        lax.fori_loop(0, 2, body, 0)
        for k in (i + 1, i):
            at = pl.ds(which * half, half)
            sib[k, which] = send(part.at[k, 1, :, :, at], from_sib.at[k, :, :, at], sibling)

    sib, first_x, first_y, second_x, second_y, home = {}, {}, {}, {}, {}, {}

    def reduce_first(i, which):
        sib[i, which].wait_recv()
        at = pl.ds(which * half, half)
        total = part[i, 0, :, :, at].astype(F32) + from_sib[i, :, :, at].astype(F32)
        pair[i, :, :, :, at] = total.astype(BF16).reshape(2, 2, tok_dev, half)
        if which == 0:
            first_x[i] = send(pair.at[i, :, 1, :, at], from_x.at[i], at_x)
        else:
            first_y[i] = send(pair.at[i, 1, :, :, at], from_y.at[i], at_y)

    def reduce_second(i):
        first_x[i].wait_recv()
        half_x[i] = (pair[i, :, 0, :, :half].astype(F32) + from_x[i].astype(F32)).astype(BF16)
        second_y[i] = send(half_x.at[i, 1], from_y2.at[i], at_y)
        first_y[i].wait_recv()
        half_y[i] = (pair[i, 0, :, :, half:].astype(F32) + from_y[i].astype(F32)).astype(BF16)
        second_x[i] = send(half_y.at[i, 1], from_x2.at[i], at_x)

    def reduce_third(i):
        second_y[i].wait_recv()
        second_x[i].wait_recv()
        left = half_x[i, 0].astype(F32) + from_y2[i].astype(F32)
        right = half_y[i, 0].astype(F32) + from_x2[i].astype(F32)
        plane[i, :, :half] = left.astype(BF16)
        plane[i, :, half:] = right.astype(BF16)
        if i:
            home[i] = send(plane.at[i], from_z.at[i - 1], at_z[i])

    spread(0)
    for i in (1, 2, 3):
        along_z[i] = send(rows.at[0, 0, 0], rows.at[i, 0, 0], at_z[i])
    for i in (1, 2):
        along_z[i].wait_recv()
        spread(i)
        relay(i - 1)
    close(0)
    along_z[3].wait_recv()
    spread(3)
    close(1)
    relay(2)
    arrived(0)
    arrived(1)
    expand(0)
    for load in loads:
        load.wait()
    forward()
    relay(3)
    close(2)
    back(0, 0)
    back(0, 1)
    close(3)
    for i in (1, 0):
        reduce_first(i, 0)
        reduce_first(i, 1)
    arrived(2)
    arrived(3)
    expand(2)
    forward()
    reduce_second(1)
    reduce_second(0)
    back(2, 0)
    reduce_third(1)
    reduce_third(0)
    back(2, 1)
    for which in (0, 1):
        reduce_first(3, which)
        reduce_first(2, which)
    for i in (3, 2):
        reduce_second(i)
    for i in (3, 2):
        reduce_third(i)
    total = plane[0].astype(F32)
    for i in (1, 2, 3):
        home[i].wait_recv()
        total += from_z[i - 1].astype(F32)
    out_ref[...] = total.astype(BF16)
    for copy in copies:
        copy.wait_send()


def dense(tokens, cotangent, gates, routes, w_gate, w_up, w_down):
    tok_dev, width = tokens.shape
    padded = -(-w_gate.shape[1] // TILE) * TILE
    blocks = lax.axis_size("hid") // EXP_DEV
    count = 2 * CORES * 4 * tok_dev
    half = width // 2
    top = gates.shape[1]
    hbm = pl.BlockSpec(memory_space=pltpu.HBM)
    copies = 62
    return pl.pallas_call(
        functools.partial(dense_kernel, blocks),
        out_shape=jax.ShapeDtypeStruct((tok_dev, width), BF16),
        in_specs=[hbm] * 7,
        out_specs=pl.BlockSpec(memory_space=pltpu.VMEM),
        scratch_shapes=[
            pltpu.VMEM((4, CORES, 4, tok_dev, 2 * width + LANES), BF16),
            pltpu.VMEM((top, tok_dev), F32),
            pltpu.VMEM((top, tok_dev), jnp.int32),
            pltpu.VMEM((padded, width), BF16),
            pltpu.VMEM((padded, width), BF16),
            pltpu.VMEM((padded, width), BF16),
            pltpu.VMEM((count, width), BF16),
            pltpu.VMEM((count, width), BF16),
            pltpu.VMEM((count, padded), BF16),
            pltpu.VMEM((count, padded), BF16),
            pltpu.VMEM((4, CORES, 4, tok_dev, width), BF16),
            pltpu.VMEM((4, 4, tok_dev, width), BF16),
            pltpu.VMEM((4, 2, 2, tok_dev, width), BF16),
            pltpu.VMEM((4, 2, tok_dev, half), BF16),
            pltpu.VMEM((4, 2, tok_dev, half), BF16),
            pltpu.VMEM((4, 2, tok_dev, half), BF16),
            pltpu.VMEM((4, 2, tok_dev, half), BF16),
            pltpu.VMEM((4, tok_dev, half), BF16),
            pltpu.VMEM((4, tok_dev, half), BF16),
            pltpu.VMEM((4, tok_dev, width), BF16),
            pltpu.VMEM((3, tok_dev, width), BF16),
            pltpu.SemaphoreType.DMA((4,)),
            pltpu.SemaphoreType.DMA((3,)),
            pltpu.SemaphoreType.DMA((copies,)),
            pltpu.SemaphoreType.DMA((copies,)),
        ],
        compiler_params=pltpu.CompilerParams(
            collective_id=0, has_side_effects=True, vmem_limit_bytes=60 * 1024 * 1024
        ),
    )(tokens, cotangent, gates.T, routes.T, w_gate, w_up, w_down)


def hidden_grad(inputs, cotan, wgate, wup, wdown):
    dims = (((1,), (1,)), ((), ()))
    gate = lax.dot_general(inputs, wgate, dims, preferred_element_type=jnp.float32)
    upper = lax.dot_general(inputs, wup, dims, preferred_element_type=jnp.float32)
    hidden = lax.dot_general(cotan, wdown, dims, preferred_element_type=jnp.float32)
    sig = jax.nn.sigmoid(gate)
    d_up = (hidden * gate * sig).astype(jnp.bfloat16)
    d_gate = (hidden * upper * sig * (1.0 + gate * (1.0 - sig))).astype(jnp.bfloat16)
    first = jnp.dot(d_gate, wgate, preferred_element_type=jnp.float32)
    second = jnp.dot(d_up, wup, preferred_element_type=jnp.float32)
    return first + second


def per_device(tokens, cotangent, gates, routes, w_gate, w_up, w_down):
    n_ex = lax.axis_size("ex")
    n_hid = lax.axis_size("hid")
    tok_dev, width = tokens.shape
    top = routes.shape[1]
    experts_all = EXP_DEV * n_ex
    blocks = n_hid // EXP_DEV
    slot_cap = max(2, (2 * tok_dev * top + experts_all - 1) // experts_all)
    flat = routes.reshape(-1)
    count = flat.shape[0]
    order = jnp.arange(count, dtype=jnp.int32)
    same = flat[:, None] == flat[None, :]
    earlier = order[None, :] < order[:, None]
    slot = jnp.sum(jnp.where(same & earlier, 1, 0), axis=1).astype(jnp.int32)
    owner_ex = flat // EXP_DEV
    local = flat % EXP_DEV
    rows_x = jnp.repeat(tokens, top, axis=0)
    rows_dy = jnp.repeat(cotangent, top, axis=0).astype(jnp.float32)
    scaled = (gates.reshape(-1)[:, None] * rows_dy).astype(jnp.bfloat16)
    stacked = jnp.stack([rows_x, scaled], axis=1)
    buffer = (
        jnp.zeros((EXP_DEV, 2, n_ex, slot_cap, width), jnp.bfloat16)
        .at[local, :, owner_ex, slot]
        .set(stacked)
    )
    arrived = lax.all_to_all(buffer, "ex", split_axis=2, concat_axis=2, tiled=True)
    tail = arrived.shape[1:]
    received = lax.all_to_all(
        jnp.broadcast_to(arrived[:, None], (EXP_DEV, blocks) + tail).reshape((n_hid,) + tail),
        "hid",
        split_axis=0,
        concat_axis=0,
        tiled=True,
    )
    rows = n_hid * n_ex * slot_cap
    inputs = received[:, 0].reshape(rows, width)
    cotan = received[:, 1].reshape(rows, width)
    partial_value = hidden_grad(inputs, cotan, w_gate[0], w_up[0], w_down[0]).astype(jnp.bfloat16)
    partial_value = partial_value.reshape(n_hid, n_ex, slot_cap, width)
    moved = lax.all_to_all(partial_value, "ex", split_axis=1, concat_axis=1, tiled=True)
    landed = lax.all_to_all(moved, "hid", split_axis=0, concat_axis=0, tiled=True)
    back = jnp.sum(
        landed.astype(jnp.float32).reshape(EXP_DEV, blocks, n_ex, slot_cap, width), axis=1
    ).astype(jnp.bfloat16)
    index = (local * n_ex + owner_ex) * slot_cap + slot
    picked = back.reshape(-1, width)[index].reshape(tok_dev, top, width).astype(jnp.float32)
    return jnp.sum(picked, axis=1).astype(jnp.bfloat16)


def solution(mesh):
    in_specs = (
        P(("ex", "hid"), None),
        P(("ex", "hid"), None),
        P(("ex", "hid"), None),
        P(("ex", "hid"), None),
        P(("ex", "hid"), None, None),
        P(("ex", "hid"), None, None),
        P(("ex", "hid"), None, None),
    )
    out_specs = P(("ex", "hid"), None)
    small = mesh.shape["ex"] == 4 * CORES and mesh.shape["hid"] == 4
    return jax.shard_map(
        dense if small else per_device, mesh=mesh, in_specs=in_specs, out_specs=out_specs, check_vma=False
    )
```

```python
import functools

import jax
import jax.numpy as jnp
from jax import lax
from jax.experimental import pallas as pl
from jax.experimental.pallas import tpu as pltpu
from jax.sharding import PartitionSpec as P

EXP_DEV = 2
CORES = 2
LANES = 128
TILE = 256
F32 = jnp.float32
BF16 = jnp.bfloat16


def dense_kernel(
    blocks, tok_ref, cot_ref, gates_ref, routes_ref, wg_hbm, wu_hbm, wd_hbm, out_ref,
    rows, small_g, small_r, wg, wu, wd, xs, ys, dgs, dus, part, from_sib, pair, from_x, from_y,
    half_x, half_y, from_y2, from_x2, plane, from_z, in_sem, w_sem, send_sem, recv_sem,
):
    tok_dev, width = tok_ref.shape
    top = gates_ref.shape[0]
    units = wg_hbm.shape[1]
    half = width // 2
    ex, hid = lax.axis_index("ex"), lax.axis_index("hid")
    z, c = ex // CORES, ex % CORES
    y, x = hid // 2, hid % 2
    expert = (ex * lax.axis_size("hid") + hid) // blocks
    experts = EXP_DEV * lax.axis_size("ex")

    def device(zz, cc, yy, xx):
        return (zz * CORES + cc, yy * 2 + xx)

    z_of = (z, z + 1 - 2 * (z % 2), (z + 2) % 4, 3 - z)
    at_x = device(z, c, y, 1 - x)
    at_y = device(z, c, 1 - y, x)
    sibling = device(z, 1 - c, y, x)
    at_z = [device(zz, c, y, x) for zz in z_of]
    partners = [at_x, at_y, sibling] + at_z[1:]
    barrier = pltpu.get_barrier_semaphore()
    for partner in partners:
        pl.semaphore_signal(barrier, inc=1, device_id=partner, device_id_type=pl.DeviceIdType.MESH)

    first = [
        pltpu.make_async_copy(src, dst, in_sem.at[i])
        for i, (src, dst) in enumerate(
            (
                (gates_ref, small_g),
                (routes_ref, small_r),
                (tok_ref, rows.at[0, 0, 0, :, pl.ds(0, width)]),
                (cot_ref, rows.at[0, 0, 0, :, pl.ds(width, width)]),
            )
        )
    ]
    for load in first:
        load.start()
    loads = [
        pltpu.make_async_copy(src.at[0], dst.at[pl.ds(0, units)], w_sem.at[i])
        for i, (src, dst) in enumerate(((wg_hbm, wg), (wu_hbm, wu), (wd_hbm, wd)))
    ]
    for load in loads:
        load.start()
    padded = wg.shape[0]
    for weight in (wg, wu, wd):
        weight[units:] = jnp.zeros((padded - units, width), BF16)

    lane = lax.broadcasted_iota(jnp.int32, (tok_dev, LANES), 1)
    dense = jnp.zeros((tok_dev, LANES), F32)
    diagonal = lax.broadcasted_iota(jnp.int32, (tok_dev, tok_dev), 0) == lax.broadcasted_iota(
        jnp.int32, (tok_dev, tok_dev), 1
    )
    place = (lane % experts).astype(F32)
    first[0].wait()
    first[1].wait()
    for k in range(top):
        gate_k = jnp.sum(jnp.where(diagonal, small_g[k : k + 1, :], 0.0), axis=1, keepdims=True)
        route_k = jnp.sum(jnp.where(diagonal, small_r[k : k + 1, :].astype(F32), 0.0), axis=1, keepdims=True)
        dense += jnp.where(place == route_k, gate_k, 0.0)
    high = dense.astype(BF16).astype(F32)
    rest = dense - high
    mid = rest.astype(BF16).astype(F32)
    low = rest - mid
    term = lane // experts
    terms = jnp.where(term == 0, high, jnp.where(term == 1, mid, jnp.where(term == 2, low, 0.0)))
    rows[0, 0, 0, :, 2 * width :] = terms.astype(BF16)
    first[2].wait()
    first[3].wait()
    pl.semaphore_wait(barrier, len(partners))

    copies = []

    def send(src, dst, target):
        k = len(copies)
        copy = pltpu.make_async_remote_copy(
            src_ref=src, dst_ref=dst, send_sem=send_sem.at[k], recv_sem=recv_sem.at[k],
            device_id=target, device_id_type=pl.DeviceIdType.MESH,
        )
        copy.start()
        copies.append(copy)
        return copy

    along_z, along_x, along_y, diag_x, diag_y, diag_z, cross = {}, {}, {}, {}, {}, {}, {}

    def spread(i):
        along_x[i] = send(rows.at[i, 0, 0], rows.at[i, 0, 1], at_x)
        along_y[i] = send(rows.at[i, 0, 0], rows.at[i, 0, 2], at_y)
        cross[i, 0] = send(rows.at[i, 0, 0], rows.at[i, 1, 0], sibling)

    def relay(i):
        along_x[i].wait_recv()
        if i % 2 == 0:
            diag_y[i] = send(rows.at[i, 0, 1, :, pl.ds(0, width)], rows.at[i, 0, 3, :, pl.ds(0, width)], at_y)
        cross[i, 1] = send(rows.at[i, 0, 1], rows.at[i, 1, 1], sibling)
        along_y[i].wait_recv()
        if i % 2 == 0:
            rest_of = pl.ds(width, width + LANES)
            diag_x[i] = send(rows.at[i, 0, 2, :, rest_of], rows.at[i, 0, 3, :, rest_of], at_x)
        cross[i, 2] = send(rows.at[i, 0, 2], rows.at[i, 1, 2], sibling)

    def close(i):
        if i % 2 == 0:
            diag_y[i].wait_recv()
            diag_x[i].wait_recv()
            diag_z[i + 1] = send(rows.at[i, 0, 3], rows.at[i + 1, 0, 3], at_z[1])
        else:
            diag_z[i].wait_recv()
        cross[i, 3] = send(rows.at[i, 0, 3], rows.at[i, 1, 3], sibling)

    def arrived(i):
        for r in range(4):
            cross[i, r].wait_recv()

    count = 2 * CORES * 4 * tok_dev
    rhs_last = (((1,), (1,)), ((), ()))

    def expand(i):
        gate_rows = rows[pl.ds(i, 2), :, :, :, pl.ds(2 * width, LANES)].reshape(count, LANES)
        lanes = lax.broadcasted_iota(jnp.int32, (count, LANES), 1)
        mine = (lanes % experts == expert) & (lanes < 3 * experts)
        gate = jnp.sum(jnp.where(mine, gate_rows.astype(F32), 0.0), axis=1, keepdims=True)
        cot = rows[pl.ds(i, 2), :, :, :, pl.ds(width, width)].reshape(count, width)
        ys[...] = (gate * cot.astype(F32)).astype(BF16)
        xs[...] = rows[pl.ds(i, 2), :, :, :, pl.ds(0, width)].reshape(count, width)

    def forward(low, high):
        def body(n, carry):
            at = pl.ds(pl.multiple_of(n * TILE, TILE), TILE)
            gate = lax.dot_general(xs[...], wg[at, :], rhs_last, preferred_element_type=F32)
            upper = lax.dot_general(xs[...], wu[at, :], rhs_last, preferred_element_type=F32)
            down = lax.dot_general(ys[...], wd[at, :], rhs_last, preferred_element_type=F32)
            sig = jax.nn.sigmoid(gate)
            dus[:, at] = (down * gate * sig).astype(BF16)
            dgs[:, at] = (down * upper * sig * (1.0 + gate * (1.0 - sig))).astype(BF16)
            return carry

        lax.fori_loop(low, high, body, 0)

    def back(i, which):
        step = half // 2

        def body(n, carry):
            at = pl.ds(pl.multiple_of(which * half + n * step, step), step)
            value = jnp.dot(dgs[...], wg[:, at], preferred_element_type=F32)
            value += jnp.dot(dus[...], wu[:, at], preferred_element_type=F32)
            part[pl.ds(i, 2), :, :, :, at] = value.astype(BF16).reshape(2, CORES, 4, tok_dev, step)
            return carry

        lax.fori_loop(0, 2, body, 0)
        for k in (i + 1, i):
            at = pl.ds(which * half, half)
            sib[k, which] = send(part.at[k, 1, :, :, at], from_sib.at[k, :, :, at], sibling)

    sib, first_x, first_y, second_x, second_y, home = {}, {}, {}, {}, {}, {}

    def reduce_first(i, which):
        sib[i, which].wait_recv()
        at = pl.ds(which * half, half)
        total = part[i, 0, :, :, at].astype(F32) + from_sib[i, :, :, at].astype(F32)
        pair[i, :, :, :, at] = total.astype(BF16).reshape(2, 2, tok_dev, half)
        if which == 0:
            first_x[i] = send(pair.at[i, :, 1, :, at], from_x.at[i], at_x)
        else:
            first_y[i] = send(pair.at[i, 1, :, :, at], from_y.at[i], at_y)

    def reduce_second(i):
        first_x[i].wait_recv()
        half_x[i] = (pair[i, :, 0, :, :half].astype(F32) + from_x[i].astype(F32)).astype(BF16)
        second_y[i] = send(half_x.at[i, 1], from_y2.at[i], at_y)
        first_y[i].wait_recv()
        half_y[i] = (pair[i, 0, :, :, half:].astype(F32) + from_y[i].astype(F32)).astype(BF16)
        second_x[i] = send(half_y.at[i, 1], from_x2.at[i], at_x)

    def reduce_third(i):
        second_y[i].wait_recv()
        second_x[i].wait_recv()
        left = half_x[i, 0].astype(F32) + from_y2[i].astype(F32)
        right = half_y[i, 0].astype(F32) + from_x2[i].astype(F32)
        if i == 2:
            home[3].wait_recv()
            left += from_z[2, :, :half].astype(F32)
            right += from_z[2, :, half:].astype(F32)
        plane[i, :, :half] = left.astype(BF16)
        plane[i, :, half:] = right.astype(BF16)
        if i:
            home[i] = send(plane.at[i], from_z.at[i - 1], at_z[2 if i == 2 else 1])

    tiles = padded // TILE
    spread(0)
    for i in (1, 2, 3):
        along_z[i] = send(rows.at[0, 0, 0], rows.at[i, 0, 0], at_z[i])
    along_z[1].wait_recv()
    spread(1)
    relay(0)
    relay(1)
    close(0)
    along_z[2].wait_recv()
    spread(2)
    close(1)
    relay(2)
    along_z[3].wait_recv()
    spread(3)
    arrived(0)
    arrived(1)
    expand(0)
    for load in loads:
        load.wait()
    forward(0, 1)
    close(2)
    forward(1, tiles)
    relay(3)
    back(0, 0)
    close(3)
    back(0, 1)
    for i in (1, 0):
        reduce_first(i, 0)
        reduce_first(i, 1)
    arrived(2)
    arrived(3)
    expand(2)
    forward(0, tiles)
    reduce_second(1)
    reduce_second(0)
    back(2, 0)
    reduce_third(1)
    reduce_third(0)
    back(2, 1)
    for which in (0, 1):
        reduce_first(3, which)
        reduce_first(2, which)
    for i in (3, 2):
        reduce_second(i)
    for i in (3, 2):
        reduce_third(i)
    total = plane[0].astype(F32)
    for i in (1, 2):
        home[i].wait_recv()
        total += from_z[i - 1].astype(F32)
    out_ref[...] = total.astype(BF16)
    for copy in copies:
        copy.wait_send()


def dense(tokens, cotangent, gates, routes, w_gate, w_up, w_down):
    tok_dev, width = tokens.shape
    padded = -(-w_gate.shape[1] // TILE) * TILE
    blocks = lax.axis_size("hid") // EXP_DEV
    count = 2 * CORES * 4 * tok_dev
    half = width // 2
    top = gates.shape[1]
    hbm = pl.BlockSpec(memory_space=pltpu.HBM)
    copies = 60
    return pl.pallas_call(
        functools.partial(dense_kernel, blocks),
        out_shape=jax.ShapeDtypeStruct((tok_dev, width), BF16),
        in_specs=[hbm] * 7,
        out_specs=pl.BlockSpec(memory_space=pltpu.VMEM),
        scratch_shapes=[
            pltpu.VMEM((4, CORES, 4, tok_dev, 2 * width + LANES), BF16),
            pltpu.VMEM((top, tok_dev), F32),
            pltpu.VMEM((top, tok_dev), jnp.int32),
            pltpu.VMEM((padded, width), BF16),
            pltpu.VMEM((padded, width), BF16),
            pltpu.VMEM((padded, width), BF16),
            pltpu.VMEM((count, width), BF16),
            pltpu.VMEM((count, width), BF16),
            pltpu.VMEM((count, padded), BF16),
            pltpu.VMEM((count, padded), BF16),
            pltpu.VMEM((4, CORES, 4, tok_dev, width), BF16),
            pltpu.VMEM((4, 4, tok_dev, width), BF16),
            pltpu.VMEM((4, 2, 2, tok_dev, width), BF16),
            pltpu.VMEM((4, 2, tok_dev, half), BF16),
            pltpu.VMEM((4, 2, tok_dev, half), BF16),
            pltpu.VMEM((4, 2, tok_dev, half), BF16),
            pltpu.VMEM((4, 2, tok_dev, half), BF16),
            pltpu.VMEM((4, tok_dev, half), BF16),
            pltpu.VMEM((4, tok_dev, half), BF16),
            pltpu.VMEM((4, tok_dev, width), BF16),
            pltpu.VMEM((3, tok_dev, width), BF16),
            pltpu.SemaphoreType.DMA((4,)),
            pltpu.SemaphoreType.DMA((3,)),
            pltpu.SemaphoreType.DMA((copies,)),
            pltpu.SemaphoreType.DMA((copies,)),
        ],
        compiler_params=pltpu.CompilerParams(
            collective_id=0, has_side_effects=True, vmem_limit_bytes=60 * 1024 * 1024
        ),
    )(tokens, cotangent, gates.T, routes.T, w_gate, w_up, w_down)


def hidden_grad(inputs, cotan, wgate, wup, wdown):
    dims = (((1,), (1,)), ((), ()))
    gate = lax.dot_general(inputs, wgate, dims, preferred_element_type=jnp.float32)
    upper = lax.dot_general(inputs, wup, dims, preferred_element_type=jnp.float32)
    hidden = lax.dot_general(cotan, wdown, dims, preferred_element_type=jnp.float32)
    sig = jax.nn.sigmoid(gate)
    d_up = (hidden * gate * sig).astype(jnp.bfloat16)
    d_gate = (hidden * upper * sig * (1.0 + gate * (1.0 - sig))).astype(jnp.bfloat16)
    first = jnp.dot(d_gate, wgate, preferred_element_type=jnp.float32)
    second = jnp.dot(d_up, wup, preferred_element_type=jnp.float32)
    return first + second


def per_device(tokens, cotangent, gates, routes, w_gate, w_up, w_down):
    n_ex = lax.axis_size("ex")
    n_hid = lax.axis_size("hid")
    tok_dev, width = tokens.shape
    top = routes.shape[1]
    experts_all = EXP_DEV * n_ex
    blocks = n_hid // EXP_DEV
    slot_cap = max(2, (2 * tok_dev * top + experts_all - 1) // experts_all)
    flat = routes.reshape(-1)
    count = flat.shape[0]
    order = jnp.arange(count, dtype=jnp.int32)
    same = flat[:, None] == flat[None, :]
    earlier = order[None, :] < order[:, None]
    slot = jnp.sum(jnp.where(same & earlier, 1, 0), axis=1).astype(jnp.int32)
    owner_ex = flat // EXP_DEV
    local = flat % EXP_DEV
    rows_x = jnp.repeat(tokens, top, axis=0)
    rows_dy = jnp.repeat(cotangent, top, axis=0).astype(jnp.float32)
    scaled = (gates.reshape(-1)[:, None] * rows_dy).astype(jnp.bfloat16)
    stacked = jnp.stack([rows_x, scaled], axis=1)
    buffer = (
        jnp.zeros((EXP_DEV, 2, n_ex, slot_cap, width), jnp.bfloat16)
        .at[local, :, owner_ex, slot]
        .set(stacked)
    )
    arrived = lax.all_to_all(buffer, "ex", split_axis=2, concat_axis=2, tiled=True)
    tail = arrived.shape[1:]
    received = lax.all_to_all(
        jnp.broadcast_to(arrived[:, None], (EXP_DEV, blocks) + tail).reshape((n_hid,) + tail),
        "hid",
        split_axis=0,
        concat_axis=0,
        tiled=True,
    )
    rows = n_hid * n_ex * slot_cap
    inputs = received[:, 0].reshape(rows, width)
    cotan = received[:, 1].reshape(rows, width)
    partial_value = hidden_grad(inputs, cotan, w_gate[0], w_up[0], w_down[0]).astype(jnp.bfloat16)
    partial_value = partial_value.reshape(n_hid, n_ex, slot_cap, width)
    moved = lax.all_to_all(partial_value, "ex", split_axis=1, concat_axis=1, tiled=True)
    landed = lax.all_to_all(moved, "hid", split_axis=0, concat_axis=0, tiled=True)
    back = jnp.sum(
        landed.astype(jnp.float32).reshape(EXP_DEV, blocks, n_ex, slot_cap, width), axis=1
    ).astype(jnp.bfloat16)
    index = (local * n_ex + owner_ex) * slot_cap + slot
    picked = back.reshape(-1, width)[index].reshape(tok_dev, top, width).astype(jnp.float32)
    return jnp.sum(picked, axis=1).astype(jnp.bfloat16)


def solution(mesh):
    in_specs = (
        P(("ex", "hid"), None),
        P(("ex", "hid"), None),
        P(("ex", "hid"), None),
        P(("ex", "hid"), None),
        P(("ex", "hid"), None, None),
        P(("ex", "hid"), None, None),
        P(("ex", "hid"), None, None),
    )
    out_specs = P(("ex", "hid"), None)
    small = mesh.shape["ex"] == 4 * CORES and mesh.shape["hid"] == 4
    return jax.shard_map(
        dense if small else per_device, mesh=mesh, in_specs=in_specs, out_specs=out_specs, check_vma=False
    )
```

```python
import functools

import jax
import jax.numpy as jnp
from jax import lax
from jax.experimental import pallas as pl
from jax.experimental.pallas import tpu as pltpu
from jax.sharding import PartitionSpec as P

EXP_DEV = 2
CORES = 2
LANES = 128
TILE = 256
F32 = jnp.float32
BF16 = jnp.bfloat16


def dense_kernel(
    blocks, tok_ref, cot_ref, gates_ref, routes_ref, wg_hbm, wu_hbm, wd_hbm, out_ref,
    rows, small_g, small_r, wg, wu, wd, wgt, wut, wdt, xs, ys, dgs, dus, part, from_sib, pair, from_x, from_y,
    half_x, half_y, from_y2, from_x2, plane, from_z, in_sem, w_sem, send_sem, recv_sem,
):
    tok_dev, width = tok_ref.shape
    top = gates_ref.shape[0]
    units = wg_hbm.shape[1]
    half = width // 2
    ex, hid = lax.axis_index("ex"), lax.axis_index("hid")
    z, c = ex // CORES, ex % CORES
    y, x = hid // 2, hid % 2
    expert = (ex * lax.axis_size("hid") + hid) // blocks
    experts = EXP_DEV * lax.axis_size("ex")

    first = [
        pltpu.make_async_copy(src, dst, in_sem.at[i])
        for i, (src, dst) in enumerate(
            (
                (gates_ref, small_g),
                (routes_ref, small_r),
                (tok_ref, rows.at[0, 0, 0, :, pl.ds(0, width)]),
                (cot_ref, rows.at[0, 0, 0, :, pl.ds(width, width)]),
            )
        )
    ]
    for load in first:
        load.start()
    loads = [
        pltpu.make_async_copy(src.at[0], dst.at[pl.ds(0, units)], w_sem.at[i])
        for i, (src, dst) in enumerate(((wg_hbm, wg), (wu_hbm, wu), (wd_hbm, wd)))
    ]
    for load in loads:
        load.start()
    padded = wg.shape[0]
    for weight in (wg, wu, wd):
        weight[units:] = jnp.zeros((padded - units, width), BF16)

    def device(zz, cc, yy, xx):
        return (zz * CORES + cc, yy * 2 + xx)

    z_of = (z, z + 1 - 2 * (z % 2), (z + 2) % 4, 3 - z)
    at_x = device(z, c, y, 1 - x)
    at_y = device(z, c, 1 - y, x)
    sibling = device(z, 1 - c, y, x)
    at_z = [device(zz, c, y, x) for zz in z_of]
    partners = [at_x, at_y, sibling] + at_z[1:]
    barrier = pltpu.get_barrier_semaphore()
    for partner in partners:
        pl.semaphore_signal(barrier, inc=1, device_id=partner, device_id_type=pl.DeviceIdType.MESH)

    lane = lax.broadcasted_iota(jnp.int32, (tok_dev, LANES), 1)
    dense = jnp.zeros((tok_dev, LANES), F32)
    diagonal = lax.broadcasted_iota(jnp.int32, (tok_dev, tok_dev), 0) == lax.broadcasted_iota(
        jnp.int32, (tok_dev, tok_dev), 1
    )
    place = (lane % experts).astype(F32)
    first[0].wait()
    first[1].wait()
    for k in range(top):
        gate_k = jnp.sum(jnp.where(diagonal, small_g[k : k + 1, :], 0.0), axis=1, keepdims=True)
        route_k = jnp.sum(jnp.where(diagonal, small_r[k : k + 1, :].astype(F32), 0.0), axis=1, keepdims=True)
        dense += jnp.where(place == route_k, gate_k, 0.0)
    high = dense.astype(BF16).astype(F32)
    rest = dense - high
    mid = rest.astype(BF16).astype(F32)
    low = rest - mid
    term = lane // experts
    terms = jnp.where(term == 0, high, jnp.where(term == 1, mid, jnp.where(term == 2, low, 0.0)))
    rows[0, 0, 0, :, 2 * width :] = terms.astype(BF16)
    first[2].wait()
    first[3].wait()
    pl.semaphore_wait(barrier, len(partners))

    copies = []

    def send(src, dst, target):
        k = len(copies)
        copy = pltpu.make_async_remote_copy(
            src_ref=src, dst_ref=dst, send_sem=send_sem.at[k], recv_sem=recv_sem.at[k],
            device_id=target, device_id_type=pl.DeviceIdType.MESH,
        )
        copy.start()
        copies.append(copy)
        return copy

    along_z, along_x, along_y, diag_x, diag_y, cross = [None] * 4, [None] * 4, [None] * 4, [None] * 4, [None] * 4, {}

    def spread(i):
        along_x[i] = send(rows.at[i, 0, 0], rows.at[i, 0, 1], at_x)
        along_y[i] = send(rows.at[i, 0, 0], rows.at[i, 0, 2], at_y)
        cross[i, 0] = send(rows.at[i, 0, 0], rows.at[i, 1, 0], sibling)

    def relay(i):
        along_x[i].wait_recv()
        diag_y[i] = send(rows.at[i, 0, 1, :, pl.ds(0, width)], rows.at[i, 0, 3, :, pl.ds(0, width)], at_y)
        cross[i, 1] = send(rows.at[i, 0, 1], rows.at[i, 1, 1], sibling)
        along_y[i].wait_recv()
        diag_x[i] = send(
            rows.at[i, 0, 2, :, pl.ds(width, width + LANES)], rows.at[i, 0, 3, :, pl.ds(width, width + LANES)], at_x
        )
        cross[i, 2] = send(rows.at[i, 0, 2], rows.at[i, 1, 2], sibling)

    def close(i):
        diag_y[i].wait_recv()
        diag_x[i].wait_recv()
        cross[i, 3] = send(rows.at[i, 0, 3], rows.at[i, 1, 3], sibling)

    def arrived(i):
        for r in range(4):
            cross[i, r].wait_recv()

    count = 2 * CORES * 4 * tok_dev

    def expand(i):
        gate_rows = rows[pl.ds(i, 2), :, :, :, pl.ds(2 * width, LANES)].reshape(count, LANES)
        lanes = lax.broadcasted_iota(jnp.int32, (count, LANES), 1)
        mine = (lanes % experts == expert) & (lanes < 3 * experts)
        gate = jnp.sum(jnp.where(mine, gate_rows.astype(F32), 0.0), axis=1, keepdims=True)
        cot = rows[pl.ds(i, 2), :, :, :, pl.ds(width, width)].reshape(count, width)
        ys[...] = (gate * cot.astype(F32)).astype(BF16)
        xs[...] = rows[pl.ds(i, 2), :, :, :, pl.ds(0, width)].reshape(count, width)

    def turn(k):
        loads[k].wait()
        src, dst = ((wg, wgt), (wu, wut), (wd, wdt))[k]

        def body(n, carry):
            at = pl.ds(pl.multiple_of(n * TILE, TILE), TILE)
            dst[:, at] = src[at, :].T
            return carry

        lax.fori_loop(0, padded // TILE, body, 0)

    def forward():
        def body(n, carry):
            at = pl.ds(pl.multiple_of(n * TILE, TILE), TILE)
            gate = jnp.dot(xs[...], wgt[:, at], preferred_element_type=F32)
            upper = jnp.dot(xs[...], wut[:, at], preferred_element_type=F32)
            down = jnp.dot(ys[...], wdt[:, at], preferred_element_type=F32)
            sig = jax.nn.sigmoid(gate)
            dus[:, at] = (down * gate * sig).astype(BF16)
            dgs[:, at] = (down * upper * sig * (1.0 + gate * (1.0 - sig))).astype(BF16)
            return carry

        lax.fori_loop(0, padded // TILE, body, 0)

    def back(i, which):
        step = half // 2

        def body(n, carry):
            at = pl.ds(pl.multiple_of(which * half + n * step, step), step)
            value = jnp.dot(dgs[...], wg[:, at], preferred_element_type=F32)
            value += jnp.dot(dus[...], wu[:, at], preferred_element_type=F32)
            part[pl.ds(i, 2), :, :, :, at] = value.astype(BF16).reshape(2, CORES, 4, tok_dev, step)
            return carry

        lax.fori_loop(0, 2, body, 0)
        for k in (i + 1, i):
            at = pl.ds(which * half, half)
            sib[k, which] = send(part.at[k, 1, :, :, at], from_sib.at[k, :, :, at], sibling)

    sib, first_x, first_y, second_x, second_y, home = {}, {}, {}, {}, {}, {}

    def reduce_first(i, which):
        sib[i, which].wait_recv()
        at = pl.ds(which * half, half)
        total = part[i, 0, :, :, at].astype(F32) + from_sib[i, :, :, at].astype(F32)
        pair[i, :, :, :, at] = total.astype(BF16).reshape(2, 2, tok_dev, half)
        if which == 0:
            first_x[i] = send(pair.at[i, :, 1, :, at], from_x.at[i], at_x)
        else:
            first_y[i] = send(pair.at[i, 1, :, :, at], from_y.at[i], at_y)

    def reduce_second(i):
        first_x[i].wait_recv()
        half_x[i] = (pair[i, :, 0, :, :half].astype(F32) + from_x[i].astype(F32)).astype(BF16)
        second_y[i] = send(half_x.at[i, 1], from_y2.at[i], at_y)
        first_y[i].wait_recv()
        half_y[i] = (pair[i, 0, :, :, half:].astype(F32) + from_y[i].astype(F32)).astype(BF16)
        second_x[i] = send(half_y.at[i, 1], from_x2.at[i], at_x)

    def reduce_third(i):
        second_y[i].wait_recv()
        second_x[i].wait_recv()
        left = half_x[i, 0].astype(F32) + from_y2[i].astype(F32)
        right = half_y[i, 0].astype(F32) + from_x2[i].astype(F32)
        plane[i, :, :half] = left.astype(BF16)
        plane[i, :, half:] = right.astype(BF16)
        if i:
            home[i] = send(plane.at[i], from_z.at[i - 1], at_z[i])

    spread(0)
    for i in (1, 2, 3):
        along_z[i] = send(rows.at[0, 0, 0], rows.at[i, 0, 0], at_z[i])
    turn(0)
    for i in (1, 2):
        along_z[i].wait_recv()
        spread(i)
        relay(i - 1)
        turn(i)
    close(0)
    along_z[3].wait_recv()
    spread(3)
    close(1)
    relay(2)
    arrived(0)
    arrived(1)
    expand(0)
    forward()
    relay(3)
    close(2)
    back(0, 0)
    back(0, 1)
    close(3)
    for i in (1, 0):
        reduce_first(i, 0)
        reduce_first(i, 1)
    arrived(2)
    arrived(3)
    expand(2)
    forward()
    reduce_second(1)
    reduce_second(0)
    back(2, 0)
    reduce_third(1)
    reduce_third(0)
    back(2, 1)
    for which in (0, 1):
        reduce_first(3, which)
        reduce_first(2, which)
    for i in (3, 2):
        reduce_second(i)
    for i in (3, 2):
        reduce_third(i)
    total = plane[0].astype(F32)
    for i in (1, 2, 3):
        home[i].wait_recv()
        total += from_z[i - 1].astype(F32)
    out_ref[...] = total.astype(BF16)
    for copy in copies:
        copy.wait_send()


def dense(tokens, cotangent, gates, routes, w_gate, w_up, w_down):
    tok_dev, width = tokens.shape
    padded = -(-w_gate.shape[1] // TILE) * TILE
    blocks = lax.axis_size("hid") // EXP_DEV
    count = 2 * CORES * 4 * tok_dev
    half = width // 2
    top = gates.shape[1]
    hbm = pl.BlockSpec(memory_space=pltpu.HBM)
    copies = 62
    return pl.pallas_call(
        functools.partial(dense_kernel, blocks),
        out_shape=jax.ShapeDtypeStruct((tok_dev, width), BF16),
        in_specs=[hbm] * 7,
        out_specs=pl.BlockSpec(memory_space=pltpu.VMEM),
        scratch_shapes=[
            pltpu.VMEM((4, CORES, 4, tok_dev, 2 * width + LANES), BF16),
            pltpu.VMEM((top, tok_dev), F32),
            pltpu.VMEM((top, tok_dev), jnp.int32),
            pltpu.VMEM((padded, width), BF16),
            pltpu.VMEM((padded, width), BF16),
            pltpu.VMEM((padded, width), BF16),
            pltpu.VMEM((width, padded), BF16),
            pltpu.VMEM((width, padded), BF16),
            pltpu.VMEM((width, padded), BF16),
            pltpu.VMEM((count, width), BF16),
            pltpu.VMEM((count, width), BF16),
            pltpu.VMEM((count, padded), BF16),
            pltpu.VMEM((count, padded), BF16),
            pltpu.VMEM((4, CORES, 4, tok_dev, width), BF16),
            pltpu.VMEM((4, 4, tok_dev, width), BF16),
            pltpu.VMEM((4, 2, 2, tok_dev, width), BF16),
            pltpu.VMEM((4, 2, tok_dev, half), BF16),
            pltpu.VMEM((4, 2, tok_dev, half), BF16),
            pltpu.VMEM((4, 2, tok_dev, half), BF16),
            pltpu.VMEM((4, 2, tok_dev, half), BF16),
            pltpu.VMEM((4, tok_dev, half), BF16),
            pltpu.VMEM((4, tok_dev, half), BF16),
            pltpu.VMEM((4, tok_dev, width), BF16),
            pltpu.VMEM((3, tok_dev, width), BF16),
            pltpu.SemaphoreType.DMA((4,)),
            pltpu.SemaphoreType.DMA((3,)),
            pltpu.SemaphoreType.DMA((copies,)),
            pltpu.SemaphoreType.DMA((copies,)),
        ],
        compiler_params=pltpu.CompilerParams(
            collective_id=0, has_side_effects=True, vmem_limit_bytes=60 * 1024 * 1024
        ),
    )(tokens, cotangent, gates.T, routes.T, w_gate, w_up, w_down)


def hidden_grad(inputs, cotan, wgate, wup, wdown):
    dims = (((1,), (1,)), ((), ()))
    gate = lax.dot_general(inputs, wgate, dims, preferred_element_type=jnp.float32)
    upper = lax.dot_general(inputs, wup, dims, preferred_element_type=jnp.float32)
    hidden = lax.dot_general(cotan, wdown, dims, preferred_element_type=jnp.float32)
    sig = jax.nn.sigmoid(gate)
    d_up = (hidden * gate * sig).astype(jnp.bfloat16)
    d_gate = (hidden * upper * sig * (1.0 + gate * (1.0 - sig))).astype(jnp.bfloat16)
    first = jnp.dot(d_gate, wgate, preferred_element_type=jnp.float32)
    second = jnp.dot(d_up, wup, preferred_element_type=jnp.float32)
    return first + second


def per_device(tokens, cotangent, gates, routes, w_gate, w_up, w_down):
    n_ex = lax.axis_size("ex")
    n_hid = lax.axis_size("hid")
    tok_dev, width = tokens.shape
    top = routes.shape[1]
    experts_all = EXP_DEV * n_ex
    blocks = n_hid // EXP_DEV
    slot_cap = max(2, (2 * tok_dev * top + experts_all - 1) // experts_all)
    flat = routes.reshape(-1)
    count = flat.shape[0]
    order = jnp.arange(count, dtype=jnp.int32)
    same = flat[:, None] == flat[None, :]
    earlier = order[None, :] < order[:, None]
    slot = jnp.sum(jnp.where(same & earlier, 1, 0), axis=1).astype(jnp.int32)
    owner_ex = flat // EXP_DEV
    local = flat % EXP_DEV
    rows_x = jnp.repeat(tokens, top, axis=0)
    rows_dy = jnp.repeat(cotangent, top, axis=0).astype(jnp.float32)
    scaled = (gates.reshape(-1)[:, None] * rows_dy).astype(jnp.bfloat16)
    stacked = jnp.stack([rows_x, scaled], axis=1)
    buffer = (
        jnp.zeros((EXP_DEV, 2, n_ex, slot_cap, width), jnp.bfloat16)
        .at[local, :, owner_ex, slot]
        .set(stacked)
    )
    arrived = lax.all_to_all(buffer, "ex", split_axis=2, concat_axis=2, tiled=True)
    tail = arrived.shape[1:]
    received = lax.all_to_all(
        jnp.broadcast_to(arrived[:, None], (EXP_DEV, blocks) + tail).reshape((n_hid,) + tail),
        "hid",
        split_axis=0,
        concat_axis=0,
        tiled=True,
    )
    rows = n_hid * n_ex * slot_cap
    inputs = received[:, 0].reshape(rows, width)
    cotan = received[:, 1].reshape(rows, width)
    partial_value = hidden_grad(inputs, cotan, w_gate[0], w_up[0], w_down[0]).astype(jnp.bfloat16)
    partial_value = partial_value.reshape(n_hid, n_ex, slot_cap, width)
    moved = lax.all_to_all(partial_value, "ex", split_axis=1, concat_axis=1, tiled=True)
    landed = lax.all_to_all(moved, "hid", split_axis=0, concat_axis=0, tiled=True)
    back = jnp.sum(
        landed.astype(jnp.float32).reshape(EXP_DEV, blocks, n_ex, slot_cap, width), axis=1
    ).astype(jnp.bfloat16)
    index = (local * n_ex + owner_ex) * slot_cap + slot
    picked = back.reshape(-1, width)[index].reshape(tok_dev, top, width).astype(jnp.float32)
    return jnp.sum(picked, axis=1).astype(jnp.bfloat16)


def solution(mesh):
    in_specs = (
        P(("ex", "hid"), None),
        P(("ex", "hid"), None),
        P(("ex", "hid"), None),
        P(("ex", "hid"), None),
        P(("ex", "hid"), None, None),
        P(("ex", "hid"), None, None),
        P(("ex", "hid"), None, None),
    )
    out_specs = P(("ex", "hid"), None)
    small = mesh.shape["ex"] == 4 * CORES and mesh.shape["hid"] == 4
    return jax.shard_map(
        dense if small else per_device, mesh=mesh, in_specs=in_specs, out_specs=out_specs, check_vma=False
    )
```

```python
import functools

import jax
import jax.numpy as jnp
from jax import lax
from jax.experimental import pallas as pl
from jax.experimental.pallas import tpu as pltpu
from jax.sharding import PartitionSpec as P

EXP_DEV = 2
CORES = 2
LANES = 128
TILE = 256
F32 = jnp.float32
BF16 = jnp.bfloat16


def dense_kernel(
    blocks, tok_ref, cot_ref, gates_ref, routes_ref, wg_hbm, wu_hbm, wd_hbm, out_ref,
    rows, small_g, small_r, wg, wu, wd, wgt, wut, wdt, xs, ys, dgs, dus, part, from_sib, pair, from_x, from_y,
    half_x, half_y, from_y2, from_x2, plane, from_z, in_sem, w_sem, send_sem, recv_sem,
):
    tok_dev, width = tok_ref.shape
    top = gates_ref.shape[0]
    units = wg_hbm.shape[1]
    half = width // 2
    ex, hid = lax.axis_index("ex"), lax.axis_index("hid")
    z, c = ex // CORES, ex % CORES
    y, x = hid // 2, hid % 2
    expert = (ex * lax.axis_size("hid") + hid) // blocks
    experts = EXP_DEV * lax.axis_size("ex")

    first = [
        pltpu.make_async_copy(src, dst, in_sem.at[i])
        for i, (src, dst) in enumerate(
            (
                (gates_ref, small_g),
                (routes_ref, small_r),
                (tok_ref, rows.at[0, 0, 0, :, pl.ds(0, width)]),
                (cot_ref, rows.at[0, 0, 0, :, pl.ds(width, width)]),
            )
        )
    ]
    for load in first:
        load.start()
    loads = [
        pltpu.make_async_copy(src.at[0], dst.at[pl.ds(0, units)], w_sem.at[i])
        for i, (src, dst) in enumerate(((wg_hbm, wg), (wu_hbm, wu), (wd_hbm, wd)))
    ]
    for load in loads:
        load.start()
    padded = wg.shape[0]
    for weight in (wg, wu, wd):
        weight[units:] = jnp.zeros((padded - units, width), BF16)

    def device(zz, cc, yy, xx):
        return (zz * CORES + cc, yy * 2 + xx)

    z_of = (z, z + 1 - 2 * (z % 2), (z + 2) % 4, 3 - z)
    at_x = device(z, c, y, 1 - x)
    at_y = device(z, c, 1 - y, x)
    sibling = device(z, 1 - c, y, x)
    at_z = [device(zz, c, y, x) for zz in z_of]
    partners = [at_x, at_y, sibling] + at_z[1:]
    barrier = pltpu.get_barrier_semaphore()
    for partner in partners:
        pl.semaphore_signal(barrier, inc=1, device_id=partner, device_id_type=pl.DeviceIdType.MESH)

    lane = lax.broadcasted_iota(jnp.int32, (tok_dev, LANES), 1)
    dense = jnp.zeros((tok_dev, LANES), F32)
    diagonal = lax.broadcasted_iota(jnp.int32, (tok_dev, tok_dev), 0) == lax.broadcasted_iota(
        jnp.int32, (tok_dev, tok_dev), 1
    )
    place = (lane % experts).astype(F32)
    first[0].wait()
    first[1].wait()
    for k in range(top):
        gate_k = jnp.sum(jnp.where(diagonal, small_g[k : k + 1, :], 0.0), axis=1, keepdims=True)
        route_k = jnp.sum(jnp.where(diagonal, small_r[k : k + 1, :].astype(F32), 0.0), axis=1, keepdims=True)
        dense += jnp.where(place == route_k, gate_k, 0.0)
    high = dense.astype(BF16).astype(F32)
    rest = dense - high
    mid = rest.astype(BF16).astype(F32)
    low = rest - mid
    term = lane // experts
    terms = jnp.where(term == 0, high, jnp.where(term == 1, mid, jnp.where(term == 2, low, 0.0)))
    rows[0, 0, 0, :, 2 * width :] = terms.astype(BF16)
    first[2].wait()
    first[3].wait()
    pl.semaphore_wait(barrier, len(partners))

    copies = []

    def send(src, dst, target):
        k = len(copies)
        copy = pltpu.make_async_remote_copy(
            src_ref=src, dst_ref=dst, send_sem=send_sem.at[k], recv_sem=recv_sem.at[k],
            device_id=target, device_id_type=pl.DeviceIdType.MESH,
        )
        copy.start()
        copies.append(copy)
        return copy

    along_z, along_x, along_y, diag_x, diag_y, cross = [None] * 4, [None] * 4, [None] * 4, [None] * 4, [None] * 4, {}

    def spread(i):
        along_x[i] = send(rows.at[i, 0, 0], rows.at[i, 0, 1], at_x)
        along_y[i] = send(rows.at[i, 0, 0], rows.at[i, 0, 2], at_y)
        cross[i, 0] = send(rows.at[i, 0, 0], rows.at[i, 1, 0], sibling)

    def relay(i):
        along_x[i].wait_recv()
        diag_y[i] = send(rows.at[i, 0, 1, :, pl.ds(0, width)], rows.at[i, 0, 3, :, pl.ds(0, width)], at_y)
        cross[i, 1] = send(rows.at[i, 0, 1], rows.at[i, 1, 1], sibling)
        along_y[i].wait_recv()
        diag_x[i] = send(
            rows.at[i, 0, 2, :, pl.ds(width, width + LANES)], rows.at[i, 0, 3, :, pl.ds(width, width + LANES)], at_x
        )
        cross[i, 2] = send(rows.at[i, 0, 2], rows.at[i, 1, 2], sibling)

    def close(i):
        diag_y[i].wait_recv()
        diag_x[i].wait_recv()
        cross[i, 3] = send(rows.at[i, 0, 3], rows.at[i, 1, 3], sibling)

    def arrived(i):
        for r in range(4):
            cross[i, r].wait_recv()

    count = CORES * 4 * tok_dev

    def expand(i):
        gate_rows = rows[i, :, :, :, pl.ds(2 * width, LANES)].reshape(count, LANES)
        lanes = lax.broadcasted_iota(jnp.int32, (count, LANES), 1)
        mine = (lanes % experts == expert) & (lanes < 3 * experts)
        gate = jnp.sum(jnp.where(mine, gate_rows.astype(F32), 0.0), axis=1, keepdims=True)
        cot = rows[i, :, :, :, pl.ds(width, width)].reshape(count, width)
        ys[...] = (gate * cot.astype(F32)).astype(BF16)
        xs[...] = rows[i, :, :, :, pl.ds(0, width)].reshape(count, width)

    def turn(k):
        loads[k].wait()
        src, dst = ((wg, wgt), (wu, wut), (wd, wdt))[k]

        def body(n, carry):
            at = pl.ds(pl.multiple_of(n * TILE, TILE), TILE)
            dst[:, at] = src[at, :].T
            return carry

        lax.fori_loop(0, padded // TILE, body, 0)

    def forward():
        def body(n, carry):
            at = pl.ds(pl.multiple_of(n * TILE, TILE), TILE)
            gate = jnp.dot(xs[...], wgt[:, at], preferred_element_type=F32)
            upper = jnp.dot(xs[...], wut[:, at], preferred_element_type=F32)
            down = jnp.dot(ys[...], wdt[:, at], preferred_element_type=F32)
            sig = jax.nn.sigmoid(gate)
            dus[:, at] = (down * gate * sig).astype(BF16)
            dgs[:, at] = (down * upper * sig * (1.0 + gate * (1.0 - sig))).astype(BF16)
            return carry

        lax.fori_loop(0, padded // TILE, body, 0)

    def back(i, which):
        step = half // 2

        def body(n, carry):
            at = pl.ds(pl.multiple_of(which * half + n * step, step), step)
            value = jnp.dot(dgs[...], wg[:, at], preferred_element_type=F32)
            value += jnp.dot(dus[...], wu[:, at], preferred_element_type=F32)
            part[i, :, :, :, at] = value.astype(BF16).reshape(CORES, 4, tok_dev, step)
            return carry

        lax.fori_loop(0, 2, body, 0)
        at = pl.ds(which * half, half)
        sib[i, which] = send(part.at[i, 1, :, :, at], from_sib.at[i, :, :, at], sibling)

    sib, first_x, first_y, second_x, second_y, home = {}, {}, {}, {}, {}, {}

    def reduce_first(i, which):
        sib[i, which].wait_recv()
        at = pl.ds(which * half, half)
        total = part[i, 0, :, :, at].astype(F32) + from_sib[i, :, :, at].astype(F32)
        pair[i, :, :, :, at] = total.astype(BF16).reshape(2, 2, tok_dev, half)
        if which == 0:
            first_x[i] = send(pair.at[i, :, 1, :, at], from_x.at[i], at_x)
        else:
            first_y[i] = send(pair.at[i, 1, :, :, at], from_y.at[i], at_y)

    def reduce_second(i):
        first_x[i].wait_recv()
        half_x[i] = (pair[i, :, 0, :, :half].astype(F32) + from_x[i].astype(F32)).astype(BF16)
        second_y[i] = send(half_x.at[i, 1], from_y2.at[i], at_y)
        first_y[i].wait_recv()
        half_y[i] = (pair[i, 0, :, :, half:].astype(F32) + from_y[i].astype(F32)).astype(BF16)
        second_x[i] = send(half_y.at[i, 1], from_x2.at[i], at_x)

    def reduce_third(i):
        second_y[i].wait_recv()
        second_x[i].wait_recv()
        left = half_x[i, 0].astype(F32) + from_y2[i].astype(F32)
        right = half_y[i, 0].astype(F32) + from_x2[i].astype(F32)
        plane[i, :, :half] = left.astype(BF16)
        plane[i, :, half:] = right.astype(BF16)
        if i:
            home[i] = send(plane.at[i], from_z.at[i - 1], at_z[i])

    def products(i):
        arrived(i)
        expand(i)
        forward()
        back(i, 0)
        back(i, 1)

    spread(0)
    for i in (1, 2, 3):
        along_z[i] = send(rows.at[0, 0, 0], rows.at[i, 0, 0], at_z[i])
    turn(0)
    for i in (1, 2):
        along_z[i].wait_recv()
        spread(i)
        relay(i - 1)
        turn(i)
    close(0)
    products(0)
    along_z[3].wait_recv()
    spread(3)
    close(1)
    relay(2)
    products(1)
    close(2)
    relay(3)
    for which in (0, 1):
        reduce_first(0, which)
    products(2)
    close(3)
    for which in (0, 1):
        reduce_first(1, which)
    reduce_second(0)
    for which in (0, 1):
        reduce_first(2, which)
    products(3)
    reduce_second(1)
    reduce_second(2)
    for which in (0, 1):
        reduce_first(3, which)
    for i in (1, 2):
        reduce_third(i)
    reduce_second(3)
    reduce_third(3)
    reduce_third(0)
    total = plane[0].astype(F32)
    for i in (1, 2, 3):
        home[i].wait_recv()
        total += from_z[i - 1].astype(F32)
    out_ref[...] = total.astype(BF16)
    for copy in copies:
        copy.wait_send()


def dense(tokens, cotangent, gates, routes, w_gate, w_up, w_down):
    tok_dev, width = tokens.shape
    padded = -(-w_gate.shape[1] // TILE) * TILE
    blocks = lax.axis_size("hid") // EXP_DEV
    count = CORES * 4 * tok_dev
    half = width // 2
    top = gates.shape[1]
    hbm = pl.BlockSpec(memory_space=pltpu.HBM)
    copies = 62
    return pl.pallas_call(
        functools.partial(dense_kernel, blocks),
        out_shape=jax.ShapeDtypeStruct((tok_dev, width), BF16),
        in_specs=[hbm] * 7,
        out_specs=pl.BlockSpec(memory_space=pltpu.VMEM),
        scratch_shapes=[
            pltpu.VMEM((4, CORES, 4, tok_dev, 2 * width + LANES), BF16),
            pltpu.VMEM((top, tok_dev), F32),
            pltpu.VMEM((top, tok_dev), jnp.int32),
            pltpu.VMEM((padded, width), BF16),
            pltpu.VMEM((padded, width), BF16),
            pltpu.VMEM((padded, width), BF16),
            pltpu.VMEM((width, padded), BF16),
            pltpu.VMEM((width, padded), BF16),
            pltpu.VMEM((width, padded), BF16),
            pltpu.VMEM((count, width), BF16),
            pltpu.VMEM((count, width), BF16),
            pltpu.VMEM((count, padded), BF16),
            pltpu.VMEM((count, padded), BF16),
            pltpu.VMEM((4, CORES, 4, tok_dev, width), BF16),
            pltpu.VMEM((4, 4, tok_dev, width), BF16),
            pltpu.VMEM((4, 2, 2, tok_dev, width), BF16),
            pltpu.VMEM((4, 2, tok_dev, half), BF16),
            pltpu.VMEM((4, 2, tok_dev, half), BF16),
            pltpu.VMEM((4, 2, tok_dev, half), BF16),
            pltpu.VMEM((4, 2, tok_dev, half), BF16),
            pltpu.VMEM((4, tok_dev, half), BF16),
            pltpu.VMEM((4, tok_dev, half), BF16),
            pltpu.VMEM((4, tok_dev, width), BF16),
            pltpu.VMEM((3, tok_dev, width), BF16),
            pltpu.SemaphoreType.DMA((4,)),
            pltpu.SemaphoreType.DMA((3,)),
            pltpu.SemaphoreType.DMA((copies,)),
            pltpu.SemaphoreType.DMA((copies,)),
        ],
        compiler_params=pltpu.CompilerParams(
            collective_id=0, has_side_effects=True, vmem_limit_bytes=60 * 1024 * 1024
        ),
    )(tokens, cotangent, gates.T, routes.T, w_gate, w_up, w_down)


def hidden_grad(inputs, cotan, wgate, wup, wdown):
    dims = (((1,), (1,)), ((), ()))
    gate = lax.dot_general(inputs, wgate, dims, preferred_element_type=jnp.float32)
    upper = lax.dot_general(inputs, wup, dims, preferred_element_type=jnp.float32)
    hidden = lax.dot_general(cotan, wdown, dims, preferred_element_type=jnp.float32)
    sig = jax.nn.sigmoid(gate)
    d_up = (hidden * gate * sig).astype(jnp.bfloat16)
    d_gate = (hidden * upper * sig * (1.0 + gate * (1.0 - sig))).astype(jnp.bfloat16)
    first = jnp.dot(d_gate, wgate, preferred_element_type=jnp.float32)
    second = jnp.dot(d_up, wup, preferred_element_type=jnp.float32)
    return first + second


def per_device(tokens, cotangent, gates, routes, w_gate, w_up, w_down):
    n_ex = lax.axis_size("ex")
    n_hid = lax.axis_size("hid")
    tok_dev, width = tokens.shape
    top = routes.shape[1]
    experts_all = EXP_DEV * n_ex
    blocks = n_hid // EXP_DEV
    slot_cap = max(2, (2 * tok_dev * top + experts_all - 1) // experts_all)
    flat = routes.reshape(-1)
    count = flat.shape[0]
    order = jnp.arange(count, dtype=jnp.int32)
    same = flat[:, None] == flat[None, :]
    earlier = order[None, :] < order[:, None]
    slot = jnp.sum(jnp.where(same & earlier, 1, 0), axis=1).astype(jnp.int32)
    owner_ex = flat // EXP_DEV
    local = flat % EXP_DEV
    rows_x = jnp.repeat(tokens, top, axis=0)
    rows_dy = jnp.repeat(cotangent, top, axis=0).astype(jnp.float32)
    scaled = (gates.reshape(-1)[:, None] * rows_dy).astype(jnp.bfloat16)
    stacked = jnp.stack([rows_x, scaled], axis=1)
    buffer = (
        jnp.zeros((EXP_DEV, 2, n_ex, slot_cap, width), jnp.bfloat16)
        .at[local, :, owner_ex, slot]
        .set(stacked)
    )
    arrived = lax.all_to_all(buffer, "ex", split_axis=2, concat_axis=2, tiled=True)
    tail = arrived.shape[1:]
    received = lax.all_to_all(
        jnp.broadcast_to(arrived[:, None], (EXP_DEV, blocks) + tail).reshape((n_hid,) + tail),
        "hid",
        split_axis=0,
        concat_axis=0,
        tiled=True,
    )
    rows = n_hid * n_ex * slot_cap
    inputs = received[:, 0].reshape(rows, width)
    cotan = received[:, 1].reshape(rows, width)
    partial_value = hidden_grad(inputs, cotan, w_gate[0], w_up[0], w_down[0]).astype(jnp.bfloat16)
    partial_value = partial_value.reshape(n_hid, n_ex, slot_cap, width)
    moved = lax.all_to_all(partial_value, "ex", split_axis=1, concat_axis=1, tiled=True)
    landed = lax.all_to_all(moved, "hid", split_axis=0, concat_axis=0, tiled=True)
    back = jnp.sum(
        landed.astype(jnp.float32).reshape(EXP_DEV, blocks, n_ex, slot_cap, width), axis=1
    ).astype(jnp.bfloat16)
    index = (local * n_ex + owner_ex) * slot_cap + slot
    picked = back.reshape(-1, width)[index].reshape(tok_dev, top, width).astype(jnp.float32)
    return jnp.sum(picked, axis=1).astype(jnp.bfloat16)


def solution(mesh):
    in_specs = (
        P(("ex", "hid"), None),
        P(("ex", "hid"), None),
        P(("ex", "hid"), None),
        P(("ex", "hid"), None),
        P(("ex", "hid"), None, None),
        P(("ex", "hid"), None, None),
        P(("ex", "hid"), None, None),
    )
    out_specs = P(("ex", "hid"), None)
    small = mesh.shape["ex"] == 4 * CORES and mesh.shape["hid"] == 4
    return jax.shard_map(
        dense if small else per_device, mesh=mesh, in_specs=in_specs, out_specs=out_specs, check_vma=False
    )
```

```python
import functools

import jax
import jax.numpy as jnp
from jax import lax
from jax.experimental import pallas as pl
from jax.experimental.pallas import tpu as pltpu
from jax.sharding import PartitionSpec as P

EXP_DEV = 2
CORES = 2
LANES = 128
TILE = 256
F32 = jnp.float32
BF16 = jnp.bfloat16


def dense_kernel(
    blocks, tok_ref, cot_ref, gates_ref, routes_ref, wg_hbm, wu_hbm, wd_hbm, out_ref,
    rows, small_g, small_r, wg, wu, wd, wgt, wut, wdt, xs, ys, dgs, dus, part, from_sib, pair, from_x, from_y,
    half_x, half_y, from_y2, from_x2, plane, from_z, in_sem, w_sem, send_sem, recv_sem,
):
    tok_dev, width = tok_ref.shape
    top = gates_ref.shape[0]
    units = wg_hbm.shape[1]
    half = width // 2
    ex, hid = lax.axis_index("ex"), lax.axis_index("hid")
    z, c = ex // CORES, ex % CORES
    y, x = hid // 2, hid % 2
    expert = (ex * lax.axis_size("hid") + hid) // blocks
    experts = EXP_DEV * lax.axis_size("ex")

    first = [
        pltpu.make_async_copy(src, dst, in_sem.at[i])
        for i, (src, dst) in enumerate(
            (
                (gates_ref, small_g),
                (routes_ref, small_r),
                (tok_ref, rows.at[0, 0, 0, :, pl.ds(0, width)]),
                (cot_ref, rows.at[0, 0, 0, :, pl.ds(width, width)]),
            )
        )
    ]
    for load in first:
        load.start()
    loads = [
        pltpu.make_async_copy(src.at[0], dst.at[pl.ds(0, units)], w_sem.at[i])
        for i, (src, dst) in enumerate(((wg_hbm, wg), (wu_hbm, wu), (wd_hbm, wd)))
    ]
    for load in loads:
        load.start()
    padded = wg.shape[0]
    for weight in (wg, wu, wd):
        weight[units:] = jnp.zeros((padded - units, width), BF16)

    def device(zz, cc, yy, xx):
        return (zz * CORES + cc, yy * 2 + xx)

    z_of = (z, (z + 2) % 4, 3 - z, z + 1 - 2 * (z % 2))
    at_x = device(z, c, y, 1 - x)
    at_y = device(z, c, 1 - y, x)
    sibling = device(z, 1 - c, y, x)
    at_z = [device(zz, c, y, x) for zz in z_of]
    partners = [at_x, at_y, sibling] + at_z[1:]
    barrier = pltpu.get_barrier_semaphore()
    for partner in partners:
        pl.semaphore_signal(barrier, inc=1, device_id=partner, device_id_type=pl.DeviceIdType.MESH)

    lane = lax.broadcasted_iota(jnp.int32, (tok_dev, LANES), 1)
    dense = jnp.zeros((tok_dev, LANES), F32)
    diagonal = lax.broadcasted_iota(jnp.int32, (tok_dev, tok_dev), 0) == lax.broadcasted_iota(
        jnp.int32, (tok_dev, tok_dev), 1
    )
    place = (lane % experts).astype(F32)
    first[0].wait()
    first[1].wait()
    for k in range(top):
        gate_k = jnp.sum(jnp.where(diagonal, small_g[k : k + 1, :], 0.0), axis=1, keepdims=True)
        route_k = jnp.sum(jnp.where(diagonal, small_r[k : k + 1, :].astype(F32), 0.0), axis=1, keepdims=True)
        dense += jnp.where(place == route_k, gate_k, 0.0)
    high = dense.astype(BF16).astype(F32)
    rest = dense - high
    mid = rest.astype(BF16).astype(F32)
    low = rest - mid
    term = lane // experts
    terms = jnp.where(term == 0, high, jnp.where(term == 1, mid, jnp.where(term == 2, low, 0.0)))
    rows[0, 0, 0, :, 2 * width :] = terms.astype(BF16)
    first[2].wait()
    first[3].wait()
    pl.semaphore_wait(barrier, len(partners))

    copies = []

    def send(src, dst, target):
        k = len(copies)
        copy = pltpu.make_async_remote_copy(
            src_ref=src, dst_ref=dst, send_sem=send_sem.at[k], recv_sem=recv_sem.at[k],
            device_id=target, device_id_type=pl.DeviceIdType.MESH,
        )
        copy.start()
        copies.append(copy)
        return copy

    along_z, along_x, along_y, diag_x, diag_y, cross = [None] * 4, [None] * 4, [None] * 4, [None] * 4, [None] * 4, {}

    def spread(i):
        along_x[i] = send(rows.at[i, 0, 0], rows.at[i, 0, 1], at_x)
        along_y[i] = send(rows.at[i, 0, 0], rows.at[i, 0, 2], at_y)
        cross[i, 0] = send(rows.at[i, 0, 0], rows.at[i, 1, 0], sibling)

    def relay(i):
        along_x[i].wait_recv()
        diag_y[i] = send(rows.at[i, 0, 1, :, pl.ds(0, width)], rows.at[i, 0, 3, :, pl.ds(0, width)], at_y)
        cross[i, 1] = send(rows.at[i, 0, 1], rows.at[i, 1, 1], sibling)
        along_y[i].wait_recv()
        diag_x[i] = send(
            rows.at[i, 0, 2, :, pl.ds(width, width + LANES)], rows.at[i, 0, 3, :, pl.ds(width, width + LANES)], at_x
        )
        cross[i, 2] = send(rows.at[i, 0, 2], rows.at[i, 1, 2], sibling)

    def close(i):
        diag_y[i].wait_recv()
        diag_x[i].wait_recv()
        cross[i, 3] = send(rows.at[i, 0, 3], rows.at[i, 1, 3], sibling)

    def arrived(i):
        for r in range(4):
            cross[i, r].wait_recv()

    count = CORES * 4 * tok_dev

    def expand(i):
        gate_rows = rows[i, :, :, :, pl.ds(2 * width, LANES)].reshape(count, LANES)
        lanes = lax.broadcasted_iota(jnp.int32, (count, LANES), 1)
        mine = (lanes % experts == expert) & (lanes < 3 * experts)
        gate = jnp.sum(jnp.where(mine, gate_rows.astype(F32), 0.0), axis=1, keepdims=True)
        cot = rows[i, :, :, :, pl.ds(width, width)].reshape(count, width)
        ys[...] = (gate * cot.astype(F32)).astype(BF16)
        xs[...] = rows[i, :, :, :, pl.ds(0, width)].reshape(count, width)

    def turn(k):
        loads[k].wait()
        src, dst = ((wg, wgt), (wu, wut), (wd, wdt))[k]

        def body(n, carry):
            at = pl.ds(pl.multiple_of(n * TILE, TILE), TILE)
            dst[:, at] = src[at, :].T
            return carry

        lax.fori_loop(0, padded // TILE, body, 0)

    def forward():
        def body(n, carry):
            at = pl.ds(pl.multiple_of(n * TILE, TILE), TILE)
            gate = jnp.dot(xs[...], wgt[:, at], preferred_element_type=F32)
            upper = jnp.dot(xs[...], wut[:, at], preferred_element_type=F32)
            down = jnp.dot(ys[...], wdt[:, at], preferred_element_type=F32)
            sig = jax.nn.sigmoid(gate)
            dus[:, at] = (down * gate * sig).astype(BF16)
            dgs[:, at] = (down * upper * sig * (1.0 + gate * (1.0 - sig))).astype(BF16)
            return carry

        lax.fori_loop(0, padded // TILE, body, 0)

    def back(i, which):
        step = half // 2

        def body(n, carry):
            at = pl.ds(pl.multiple_of(which * half + n * step, step), step)
            value = jnp.dot(dgs[...], wg[:, at], preferred_element_type=F32)
            value += jnp.dot(dus[...], wu[:, at], preferred_element_type=F32)
            part[i, :, :, :, at] = value.astype(BF16).reshape(CORES, 4, tok_dev, step)
            return carry

        lax.fori_loop(0, 2, body, 0)
        at = pl.ds(which * half, half)
        sib[i, which] = send(part.at[i, 1, :, :, at], from_sib.at[i, :, :, at], sibling)

    sib, first_x, first_y, second_x, second_y, home = {}, {}, {}, {}, {}, {}

    def reduce_first(i, which):
        sib[i, which].wait_recv()
        at = pl.ds(which * half, half)
        total = part[i, 0, :, :, at].astype(F32) + from_sib[i, :, :, at].astype(F32)
        pair[i, :, :, :, at] = total.astype(BF16).reshape(2, 2, tok_dev, half)
        if which == 0:
            first_x[i] = send(pair.at[i, :, 1, :, at], from_x.at[i], at_x)
        else:
            first_y[i] = send(pair.at[i, 1, :, :, at], from_y.at[i], at_y)

    def reduce_second(i):
        first_x[i].wait_recv()
        half_x[i] = (pair[i, :, 0, :, :half].astype(F32) + from_x[i].astype(F32)).astype(BF16)
        second_y[i] = send(half_x.at[i, 1], from_y2.at[i], at_y)
        first_y[i].wait_recv()
        half_y[i] = (pair[i, 0, :, :, half:].astype(F32) + from_y[i].astype(F32)).astype(BF16)
        second_x[i] = send(half_y.at[i, 1], from_x2.at[i], at_x)

    def reduce_third(i):
        second_y[i].wait_recv()
        second_x[i].wait_recv()
        left = half_x[i, 0].astype(F32) + from_y2[i].astype(F32)
        right = half_y[i, 0].astype(F32) + from_x2[i].astype(F32)
        plane[i, :, :half] = left.astype(BF16)
        plane[i, :, half:] = right.astype(BF16)
        if i:
            home[i] = send(plane.at[i], from_z.at[i - 1], at_z[i])

    def products(i):
        arrived(i)
        expand(i)
        forward()
        back(i, 0)
        back(i, 1)

    for i in (1, 2):
        along_z[i] = send(rows.at[0, 0, 0], rows.at[i, 0, 0], at_z[i])
    spread(0)
    along_z[3] = send(rows.at[0, 0, 0], rows.at[3, 0, 0], at_z[3])
    turn(0)
    for i in (1, 2):
        along_z[i].wait_recv()
        spread(i)
        relay(i - 1)
        turn(i)
    close(0)
    products(0)
    along_z[3].wait_recv()
    spread(3)
    close(1)
    relay(2)
    products(1)
    close(2)
    relay(3)
    for which in (0, 1):
        reduce_first(0, which)
    products(2)
    close(3)
    for which in (0, 1):
        reduce_first(1, which)
    reduce_second(0)
    for which in (0, 1):
        reduce_first(2, which)
    products(3)
    reduce_second(1)
    reduce_second(2)
    for which in (0, 1):
        reduce_first(3, which)
    for i in (1, 2):
        reduce_third(i)
    reduce_second(3)
    reduce_third(3)
    reduce_third(0)
    total = plane[0].astype(F32)
    for i in (1, 2, 3):
        home[i].wait_recv()
        total += from_z[i - 1].astype(F32)
    out_ref[...] = total.astype(BF16)
    for copy in copies:
        copy.wait_send()


def dense(tokens, cotangent, gates, routes, w_gate, w_up, w_down):
    tok_dev, width = tokens.shape
    padded = -(-w_gate.shape[1] // TILE) * TILE
    blocks = lax.axis_size("hid") // EXP_DEV
    count = CORES * 4 * tok_dev
    half = width // 2
    top = gates.shape[1]
    hbm = pl.BlockSpec(memory_space=pltpu.HBM)
    copies = 62
    return pl.pallas_call(
        functools.partial(dense_kernel, blocks),
        out_shape=jax.ShapeDtypeStruct((tok_dev, width), BF16),
        in_specs=[hbm] * 7,
        out_specs=pl.BlockSpec(memory_space=pltpu.VMEM),
        scratch_shapes=[
            pltpu.VMEM((4, CORES, 4, tok_dev, 2 * width + LANES), BF16),
            pltpu.VMEM((top, tok_dev), F32),
            pltpu.VMEM((top, tok_dev), jnp.int32),
            pltpu.VMEM((padded, width), BF16),
            pltpu.VMEM((padded, width), BF16),
            pltpu.VMEM((padded, width), BF16),
            pltpu.VMEM((width, padded), BF16),
            pltpu.VMEM((width, padded), BF16),
            pltpu.VMEM((width, padded), BF16),
            pltpu.VMEM((count, width), BF16),
            pltpu.VMEM((count, width), BF16),
            pltpu.VMEM((count, padded), BF16),
            pltpu.VMEM((count, padded), BF16),
            pltpu.VMEM((4, CORES, 4, tok_dev, width), BF16),
            pltpu.VMEM((4, 4, tok_dev, width), BF16),
            pltpu.VMEM((4, 2, 2, tok_dev, width), BF16),
            pltpu.VMEM((4, 2, tok_dev, half), BF16),
            pltpu.VMEM((4, 2, tok_dev, half), BF16),
            pltpu.VMEM((4, 2, tok_dev, half), BF16),
            pltpu.VMEM((4, 2, tok_dev, half), BF16),
            pltpu.VMEM((4, tok_dev, half), BF16),
            pltpu.VMEM((4, tok_dev, half), BF16),
            pltpu.VMEM((4, tok_dev, width), BF16),
            pltpu.VMEM((3, tok_dev, width), BF16),
            pltpu.SemaphoreType.DMA((4,)),
            pltpu.SemaphoreType.DMA((3,)),
            pltpu.SemaphoreType.DMA((copies,)),
            pltpu.SemaphoreType.DMA((copies,)),
        ],
        compiler_params=pltpu.CompilerParams(
            collective_id=0, has_side_effects=True, vmem_limit_bytes=60 * 1024 * 1024
        ),
    )(tokens, cotangent, gates.T, routes.T, w_gate, w_up, w_down)


def hidden_grad(inputs, cotan, wgate, wup, wdown):
    dims = (((1,), (1,)), ((), ()))
    gate = lax.dot_general(inputs, wgate, dims, preferred_element_type=jnp.float32)
    upper = lax.dot_general(inputs, wup, dims, preferred_element_type=jnp.float32)
    hidden = lax.dot_general(cotan, wdown, dims, preferred_element_type=jnp.float32)
    sig = jax.nn.sigmoid(gate)
    d_up = (hidden * gate * sig).astype(jnp.bfloat16)
    d_gate = (hidden * upper * sig * (1.0 + gate * (1.0 - sig))).astype(jnp.bfloat16)
    first = jnp.dot(d_gate, wgate, preferred_element_type=jnp.float32)
    second = jnp.dot(d_up, wup, preferred_element_type=jnp.float32)
    return first + second


def per_device(tokens, cotangent, gates, routes, w_gate, w_up, w_down):
    n_ex = lax.axis_size("ex")
    n_hid = lax.axis_size("hid")
    tok_dev, width = tokens.shape
    top = routes.shape[1]
    experts_all = EXP_DEV * n_ex
    blocks = n_hid // EXP_DEV
    slot_cap = max(2, (2 * tok_dev * top + experts_all - 1) // experts_all)
    flat = routes.reshape(-1)
    count = flat.shape[0]
    order = jnp.arange(count, dtype=jnp.int32)
    same = flat[:, None] == flat[None, :]
    earlier = order[None, :] < order[:, None]
    slot = jnp.sum(jnp.where(same & earlier, 1, 0), axis=1).astype(jnp.int32)
    owner_ex = flat // EXP_DEV
    local = flat % EXP_DEV
    rows_x = jnp.repeat(tokens, top, axis=0)
    rows_dy = jnp.repeat(cotangent, top, axis=0).astype(jnp.float32)
    scaled = (gates.reshape(-1)[:, None] * rows_dy).astype(jnp.bfloat16)
    stacked = jnp.stack([rows_x, scaled], axis=1)
    buffer = (
        jnp.zeros((EXP_DEV, 2, n_ex, slot_cap, width), jnp.bfloat16)
        .at[local, :, owner_ex, slot]
        .set(stacked)
    )
    arrived = lax.all_to_all(buffer, "ex", split_axis=2, concat_axis=2, tiled=True)
    tail = arrived.shape[1:]
    received = lax.all_to_all(
        jnp.broadcast_to(arrived[:, None], (EXP_DEV, blocks) + tail).reshape((n_hid,) + tail),
        "hid",
        split_axis=0,
        concat_axis=0,
        tiled=True,
    )
    rows = n_hid * n_ex * slot_cap
    inputs = received[:, 0].reshape(rows, width)
    cotan = received[:, 1].reshape(rows, width)
    partial_value = hidden_grad(inputs, cotan, w_gate[0], w_up[0], w_down[0]).astype(jnp.bfloat16)
    partial_value = partial_value.reshape(n_hid, n_ex, slot_cap, width)
    moved = lax.all_to_all(partial_value, "ex", split_axis=1, concat_axis=1, tiled=True)
    landed = lax.all_to_all(moved, "hid", split_axis=0, concat_axis=0, tiled=True)
    back = jnp.sum(
        landed.astype(jnp.float32).reshape(EXP_DEV, blocks, n_ex, slot_cap, width), axis=1
    ).astype(jnp.bfloat16)
    index = (local * n_ex + owner_ex) * slot_cap + slot
    picked = back.reshape(-1, width)[index].reshape(tok_dev, top, width).astype(jnp.float32)
    return jnp.sum(picked, axis=1).astype(jnp.bfloat16)


def solution(mesh):
    in_specs = (
        P(("ex", "hid"), None),
        P(("ex", "hid"), None),
        P(("ex", "hid"), None),
        P(("ex", "hid"), None),
        P(("ex", "hid"), None, None),
        P(("ex", "hid"), None, None),
        P(("ex", "hid"), None, None),
    )
    out_specs = P(("ex", "hid"), None)
    small = mesh.shape["ex"] == 4 * CORES and mesh.shape["hid"] == 4
    return jax.shard_map(
        dense if small else per_device, mesh=mesh, in_specs=in_specs, out_specs=out_specs, check_vma=False
    )
```

```python
import functools

import jax
import jax.numpy as jnp
from jax import lax
from jax.experimental import pallas as pl
from jax.experimental.pallas import tpu as pltpu
from jax.sharding import PartitionSpec as P

EXP_DEV = 2
CORES = 2
LANES = 128
TILE = 256
F32 = jnp.float32
BF16 = jnp.bfloat16


def dense_kernel(
    blocks, tok_ref, cot_ref, gates_ref, routes_ref, wg_hbm, wu_hbm, wd_hbm, out_ref,
    rows, small_g, small_r, wg, wu, wd, wgt, wut, wdt, xs, ys, dgs, dus, part, from_sib, pair, from_x, from_y,
    half_x, half_y, from_y2, from_x2, plane, from_z, in_sem, w_sem, send_sem, recv_sem,
):
    tok_dev, width = tok_ref.shape
    top = gates_ref.shape[0]
    units = wg_hbm.shape[1]
    half = width // 2
    ex, hid = lax.axis_index("ex"), lax.axis_index("hid")
    z, c = ex // CORES, ex % CORES
    y, x = hid // 2, hid % 2
    expert = (ex * lax.axis_size("hid") + hid) // blocks
    experts = EXP_DEV * lax.axis_size("ex")

    first = [
        pltpu.make_async_copy(src, dst, in_sem.at[i])
        for i, (src, dst) in enumerate(
            (
                (gates_ref, small_g),
                (routes_ref, small_r),
                (tok_ref, rows.at[0, 0, 0, :, pl.ds(0, width)]),
                (cot_ref, rows.at[0, 0, 0, :, pl.ds(width, width)]),
            )
        )
    ]
    for load in first:
        load.start()
    loads = [
        pltpu.make_async_copy(src.at[0], dst.at[pl.ds(0, units)], w_sem.at[i])
        for i, (src, dst) in enumerate(((wg_hbm, wg), (wu_hbm, wu), (wd_hbm, wd)))
    ]
    for load in loads:
        load.start()
    padded = wg.shape[0]
    for weight in (wg, wu, wd):
        weight[units:] = jnp.zeros((padded - units, width), BF16)

    def device(zz, cc, yy, xx):
        return (zz * CORES + cc, yy * 2 + xx)

    z_of = (z, z + 1 - 2 * (z % 2), (z + 2) % 4, 3 - z)
    at_x = device(z, c, y, 1 - x)
    at_y = device(z, c, 1 - y, x)
    sibling = device(z, 1 - c, y, x)
    at_z = [device(zz, c, y, x) for zz in z_of]
    partners = [at_x, at_y, sibling] + at_z[1:]
    barrier = pltpu.get_barrier_semaphore()
    for partner in partners:
        pl.semaphore_signal(barrier, inc=1, device_id=partner, device_id_type=pl.DeviceIdType.MESH)

    lane = lax.broadcasted_iota(jnp.int32, (tok_dev, LANES), 1)
    dense = jnp.zeros((tok_dev, LANES), F32)
    diagonal = lax.broadcasted_iota(jnp.int32, (tok_dev, tok_dev), 0) == lax.broadcasted_iota(
        jnp.int32, (tok_dev, tok_dev), 1
    )
    place = (lane % experts).astype(F32)
    first[0].wait()
    first[1].wait()
    for k in range(top):
        gate_k = jnp.sum(jnp.where(diagonal, small_g[k : k + 1, :], 0.0), axis=1, keepdims=True)
        route_k = jnp.sum(jnp.where(diagonal, small_r[k : k + 1, :].astype(F32), 0.0), axis=1, keepdims=True)
        dense += jnp.where(place == route_k, gate_k, 0.0)
    high = dense.astype(BF16).astype(F32)
    rest = dense - high
    mid = rest.astype(BF16).astype(F32)
    low = rest - mid
    term = lane // experts
    terms = jnp.where(term == 0, high, jnp.where(term == 1, mid, jnp.where(term == 2, low, 0.0)))
    rows[0, 0, 0, :, 2 * width :] = terms.astype(BF16)
    first[2].wait()
    first[3].wait()
    pl.semaphore_wait(barrier, len(partners))

    copies = []

    def send(src, dst, target):
        k = len(copies)
        copy = pltpu.make_async_remote_copy(
            src_ref=src, dst_ref=dst, send_sem=send_sem.at[k], recv_sem=recv_sem.at[k],
            device_id=target, device_id_type=pl.DeviceIdType.MESH,
        )
        copy.start()
        copies.append(copy)
        return copy

    along_z, along_x, along_y, diag_x, diag_y, cross = [None] * 4, [None] * 4, [None] * 4, [None] * 4, [None] * 4, {}

    def spread(i):
        along_x[i] = send(rows.at[i, 0, 0], rows.at[i, 0, 1], at_x)
        along_y[i] = send(rows.at[i, 0, 0], rows.at[i, 0, 2], at_y)
        cross[i, 0] = send(rows.at[i, 0, 0], rows.at[i, 1, 0], sibling)

    def relay(i):
        along_x[i].wait_recv()
        diag_y[i] = send(rows.at[i, 0, 1, :, pl.ds(0, width)], rows.at[i, 0, 3, :, pl.ds(0, width)], at_y)
        cross[i, 1] = send(rows.at[i, 0, 1], rows.at[i, 1, 1], sibling)
        along_y[i].wait_recv()
        diag_x[i] = send(
            rows.at[i, 0, 2, :, pl.ds(width, width + LANES)], rows.at[i, 0, 3, :, pl.ds(width, width + LANES)], at_x
        )
        cross[i, 2] = send(rows.at[i, 0, 2], rows.at[i, 1, 2], sibling)

    def close(i):
        diag_y[i].wait_recv()
        diag_x[i].wait_recv()
        cross[i, 3] = send(rows.at[i, 0, 3], rows.at[i, 1, 3], sibling)

    def arrived(i):
        for r in range(4):
            cross[i, r].wait_recv()

    count = CORES * 4 * tok_dev

    def expand(i):
        gate_rows = rows[i, :, :, :, pl.ds(2 * width, LANES)].reshape(count, LANES)
        lanes = lax.broadcasted_iota(jnp.int32, (count, LANES), 1)
        mine = (lanes % experts == expert) & (lanes < 3 * experts)
        gate = jnp.sum(jnp.where(mine, gate_rows.astype(F32), 0.0), axis=1, keepdims=True)
        cot = rows[i, :, :, :, pl.ds(width, width)].reshape(count, width)
        ys[...] = (gate * cot.astype(F32)).astype(BF16)
        xs[...] = rows[i, :, :, :, pl.ds(0, width)].reshape(count, width)

    def turn(k):
        loads[k].wait()
        src, dst = ((wg, wgt), (wu, wut), (wd, wdt))[k]

        def body(n, carry):
            at = pl.ds(pl.multiple_of(n * TILE, TILE), TILE)
            dst[:, at] = src[at, :].T
            return carry

        lax.fori_loop(0, padded // TILE, body, 0)

    def forward():
        def body(n, carry):
            at = pl.ds(pl.multiple_of(n * TILE, TILE), TILE)
            gate = jnp.dot(xs[...], wgt[:, at], preferred_element_type=F32)
            upper = jnp.dot(xs[...], wut[:, at], preferred_element_type=F32)
            down = jnp.dot(ys[...], wdt[:, at], preferred_element_type=F32)
            sig = jax.nn.sigmoid(gate)
            dus[:, at] = (down * gate * sig).astype(BF16)
            dgs[:, at] = (down * upper * sig * (1.0 + gate * (1.0 - sig))).astype(BF16)
            return carry

        lax.fori_loop(0, padded // TILE, body, 0)

    def back(i, which):
        step = half // 2

        def body(n, carry):
            at = pl.ds(pl.multiple_of(which * half + n * step, step), step)
            value = jnp.dot(dgs[...], wg[:, at], preferred_element_type=F32)
            value += jnp.dot(dus[...], wu[:, at], preferred_element_type=F32)
            part[i, :, :, :, at] = value.astype(BF16).reshape(CORES, 4, tok_dev, step)
            return carry

        lax.fori_loop(0, 2, body, 0)
        at = pl.ds(which * half, half)
        sib[i, which] = send(part.at[i, 1, :, :, at], from_sib.at[i, :, :, at], sibling)

    sib, first_x, first_y, second_x, second_y, home = {}, {}, {}, {}, {}, {}

    def reduce_first(i, which):
        sib[i, which].wait_recv()
        at = pl.ds(which * half, half)
        total = part[i, 0, :, :, at].astype(F32) + from_sib[i, :, :, at].astype(F32)
        pair[i, :, :, :, at] = total.astype(BF16).reshape(2, 2, tok_dev, half)
        if which == 0:
            first_x[i] = send(pair.at[i, :, 1, :, at], from_x.at[i], at_x)
        else:
            first_y[i] = send(pair.at[i, 1, :, :, at], from_y.at[i], at_y)

    def reduce_second(i):
        first_x[i].wait_recv()
        half_x[i] = (pair[i, :, 0, :, :half].astype(F32) + from_x[i].astype(F32)).astype(BF16)
        second_y[i] = send(half_x.at[i, 1], from_y2.at[i], at_y)
        first_y[i].wait_recv()
        half_y[i] = (pair[i, 0, :, :, half:].astype(F32) + from_y[i].astype(F32)).astype(BF16)
        second_x[i] = send(half_y.at[i, 1], from_x2.at[i], at_x)

    def reduce_third(i):
        second_y[i].wait_recv()
        second_x[i].wait_recv()
        left = half_x[i, 0].astype(F32) + from_y2[i].astype(F32)
        right = half_y[i, 0].astype(F32) + from_x2[i].astype(F32)
        plane[i, :, :half] = left.astype(BF16)
        plane[i, :, half:] = right.astype(BF16)
        if i:
            home[i] = send(plane.at[i], from_z.at[i - 1], at_z[i])

    def products(i):
        arrived(i)
        expand(i)
        forward()
        back(i, 0)
        back(i, 1)

    spread(0)
    for i in (1, 2, 3):
        along_z[i] = send(rows.at[0, 0, 0], rows.at[i, 0, 0], at_z[i])
    turn(0)
    for i in (1, 2):
        along_z[i].wait_recv()
        spread(i)
        relay(i - 1)
        turn(i)
    close(0)
    products(0)
    along_z[3].wait_recv()
    spread(3)
    close(1)
    relay(2)
    products(1)
    close(2)
    relay(3)
    for which in (0, 1):
        reduce_first(0, which)
    products(2)
    close(3)
    for which in (0, 1):
        reduce_first(1, which)
    reduce_second(0)
    for which in (0, 1):
        reduce_first(2, which)
    reduce_second(1)
    arrived(3)
    expand(3)
    forward()
    reduce_second(2)
    reduce_third(1)
    back(3, 0)
    back(3, 1)
    for which in (0, 1):
        reduce_first(3, which)
    reduce_third(2)
    reduce_second(3)
    reduce_third(3)
    reduce_third(0)
    total = plane[0].astype(F32)
    for i in (1, 2, 3):
        home[i].wait_recv()
        total += from_z[i - 1].astype(F32)
    out_ref[...] = total.astype(BF16)
    for copy in copies:
        copy.wait_send()


def dense(tokens, cotangent, gates, routes, w_gate, w_up, w_down):
    tok_dev, width = tokens.shape
    padded = -(-w_gate.shape[1] // TILE) * TILE
    blocks = lax.axis_size("hid") // EXP_DEV
    count = CORES * 4 * tok_dev
    half = width // 2
    top = gates.shape[1]
    hbm = pl.BlockSpec(memory_space=pltpu.HBM)
    copies = 62
    return pl.pallas_call(
        functools.partial(dense_kernel, blocks),
        out_shape=jax.ShapeDtypeStruct((tok_dev, width), BF16),
        in_specs=[hbm] * 7,
        out_specs=pl.BlockSpec(memory_space=pltpu.VMEM),
        scratch_shapes=[
            pltpu.VMEM((4, CORES, 4, tok_dev, 2 * width + LANES), BF16),
            pltpu.VMEM((top, tok_dev), F32),
            pltpu.VMEM((top, tok_dev), jnp.int32),
            pltpu.VMEM((padded, width), BF16),
            pltpu.VMEM((padded, width), BF16),
            pltpu.VMEM((padded, width), BF16),
            pltpu.VMEM((width, padded), BF16),
            pltpu.VMEM((width, padded), BF16),
            pltpu.VMEM((width, padded), BF16),
            pltpu.VMEM((count, width), BF16),
            pltpu.VMEM((count, width), BF16),
            pltpu.VMEM((count, padded), BF16),
            pltpu.VMEM((count, padded), BF16),
            pltpu.VMEM((4, CORES, 4, tok_dev, width), BF16),
            pltpu.VMEM((4, 4, tok_dev, width), BF16),
            pltpu.VMEM((4, 2, 2, tok_dev, width), BF16),
            pltpu.VMEM((4, 2, tok_dev, half), BF16),
            pltpu.VMEM((4, 2, tok_dev, half), BF16),
            pltpu.VMEM((4, 2, tok_dev, half), BF16),
            pltpu.VMEM((4, 2, tok_dev, half), BF16),
            pltpu.VMEM((4, tok_dev, half), BF16),
            pltpu.VMEM((4, tok_dev, half), BF16),
            pltpu.VMEM((4, tok_dev, width), BF16),
            pltpu.VMEM((3, tok_dev, width), BF16),
            pltpu.SemaphoreType.DMA((4,)),
            pltpu.SemaphoreType.DMA((3,)),
            pltpu.SemaphoreType.DMA((copies,)),
            pltpu.SemaphoreType.DMA((copies,)),
        ],
        compiler_params=pltpu.CompilerParams(
            collective_id=0, has_side_effects=True, vmem_limit_bytes=60 * 1024 * 1024
        ),
    )(tokens, cotangent, gates.T, routes.T, w_gate, w_up, w_down)


def hidden_grad(inputs, cotan, wgate, wup, wdown):
    dims = (((1,), (1,)), ((), ()))
    gate = lax.dot_general(inputs, wgate, dims, preferred_element_type=jnp.float32)
    upper = lax.dot_general(inputs, wup, dims, preferred_element_type=jnp.float32)
    hidden = lax.dot_general(cotan, wdown, dims, preferred_element_type=jnp.float32)
    sig = jax.nn.sigmoid(gate)
    d_up = (hidden * gate * sig).astype(jnp.bfloat16)
    d_gate = (hidden * upper * sig * (1.0 + gate * (1.0 - sig))).astype(jnp.bfloat16)
    first = jnp.dot(d_gate, wgate, preferred_element_type=jnp.float32)
    second = jnp.dot(d_up, wup, preferred_element_type=jnp.float32)
    return first + second


def per_device(tokens, cotangent, gates, routes, w_gate, w_up, w_down):
    n_ex = lax.axis_size("ex")
    n_hid = lax.axis_size("hid")
    tok_dev, width = tokens.shape
    top = routes.shape[1]
    experts_all = EXP_DEV * n_ex
    blocks = n_hid // EXP_DEV
    slot_cap = max(2, (2 * tok_dev * top + experts_all - 1) // experts_all)
    flat = routes.reshape(-1)
    count = flat.shape[0]
    order = jnp.arange(count, dtype=jnp.int32)
    same = flat[:, None] == flat[None, :]
    earlier = order[None, :] < order[:, None]
    slot = jnp.sum(jnp.where(same & earlier, 1, 0), axis=1).astype(jnp.int32)
    owner_ex = flat // EXP_DEV
    local = flat % EXP_DEV
    rows_x = jnp.repeat(tokens, top, axis=0)
    rows_dy = jnp.repeat(cotangent, top, axis=0).astype(jnp.float32)
    scaled = (gates.reshape(-1)[:, None] * rows_dy).astype(jnp.bfloat16)
    stacked = jnp.stack([rows_x, scaled], axis=1)
    buffer = (
        jnp.zeros((EXP_DEV, 2, n_ex, slot_cap, width), jnp.bfloat16)
        .at[local, :, owner_ex, slot]
        .set(stacked)
    )
    arrived = lax.all_to_all(buffer, "ex", split_axis=2, concat_axis=2, tiled=True)
    tail = arrived.shape[1:]
    received = lax.all_to_all(
        jnp.broadcast_to(arrived[:, None], (EXP_DEV, blocks) + tail).reshape((n_hid,) + tail),
        "hid",
        split_axis=0,
        concat_axis=0,
        tiled=True,
    )
    rows = n_hid * n_ex * slot_cap
    inputs = received[:, 0].reshape(rows, width)
    cotan = received[:, 1].reshape(rows, width)
    partial_value = hidden_grad(inputs, cotan, w_gate[0], w_up[0], w_down[0]).astype(jnp.bfloat16)
    partial_value = partial_value.reshape(n_hid, n_ex, slot_cap, width)
    moved = lax.all_to_all(partial_value, "ex", split_axis=1, concat_axis=1, tiled=True)
    landed = lax.all_to_all(moved, "hid", split_axis=0, concat_axis=0, tiled=True)
    back = jnp.sum(
        landed.astype(jnp.float32).reshape(EXP_DEV, blocks, n_ex, slot_cap, width), axis=1
    ).astype(jnp.bfloat16)
    index = (local * n_ex + owner_ex) * slot_cap + slot
    picked = back.reshape(-1, width)[index].reshape(tok_dev, top, width).astype(jnp.float32)
    return jnp.sum(picked, axis=1).astype(jnp.bfloat16)


def solution(mesh):
    in_specs = (
        P(("ex", "hid"), None),
        P(("ex", "hid"), None),
        P(("ex", "hid"), None),
        P(("ex", "hid"), None),
        P(("ex", "hid"), None, None),
        P(("ex", "hid"), None, None),
        P(("ex", "hid"), None, None),
    )
    out_specs = P(("ex", "hid"), None)
    small = mesh.shape["ex"] == 4 * CORES and mesh.shape["hid"] == 4
    return jax.shard_map(
        dense if small else per_device, mesh=mesh, in_specs=in_specs, out_specs=out_specs, check_vma=False
    )
```
